256 devices in a mesh: patch: 128 (over x, z, y), grp: 2 (over core).
Axes of the slice: x: 4, y: 4, z: 8, core: 2. Of those that a mesh axis runs over, the one named last changes fastest.
Arguments:
- right_side: float32 [6, 1024, 128], P(None, ('patch', 'grp')), may hold values from -40 to 40
- patch_blocks: int32 [128], P('patch'), may hold values from 4 to 8, as said below
- send_rows: int32 [128, 2, 4], P('patch'), may hold values from 0 to 7, as said below
- near_cols: int32 [1024, 10], P(('patch', 'grp')), may hold values from 0 to 15, as said below
- near_blocks: float32 [1024, 10, 128, 128], P(('patch', 'grp')), may hold values from -2 to 2
- inverses: float32 [128, 16, 128, 128], P('patch'), may hold values from -1.5 to 1.5
Outputs:
- solution: float32 [6, 1024, 128], P(None, ('patch', 'grp'))
- residual: float32 [6, 1024, 128], P(None, ('patch', 'grp'))
The draws below stay inside these ranges and needn't reach their ends.
Inputs may be any that keep to these rules, and one draw needn't show every extreme that they name: `patch_blocks`: every patch has 4 to 8 live slots; some patch has all 8 and some has 4. `send_rows`: every sent slot is live in the sending patch. `near_cols`: entry 0 of each row is the row's own slot within its patch.
All inputs are finite; a program needn't handle non-finite values.
Results may differ from the reference program's by a relative error of at most 0.0003.
Values sent between devices are 32-bit elements; how exact they have to be, the bound alone decides.
A program may use at most 64 MiB of HBM per device.

```python
import math
import jax
import jax.numpy as jnp
from jax import lax

BS = 128
NB = 4
NEAR = 10
NRHS = 6
CYCLES = 2
PB = 8
NE = 16
NBT = 1024


def patch_counts(key):
    patches = NBT // PB
    counts = jax.random.randint(jax.random.fold_in(key, 11), (patches,), NB, PB + 1)
    fullest = jax.random.randint(jax.random.fold_in(key, 12), (), 0, patches)
    lightest = (fullest + 1 + jax.random.randint(jax.random.fold_in(key, 13), (), 0, patches - 1)) % patches
    counts = counts.at[fullest].set(PB)
    return counts.at[lightest].set(NB).astype(jnp.int32)


def draw_patch_blocks(key, part):
    return patch_counts(key)


def draw_send_rows(key, part):
    counts = patch_counts(key)
    key = jax.random.fold_in(key, 2)
    return jax.random.randint(key, (NBT // PB, 2, NB), 0, counts[:, None, None]).astype(jnp.int32)


def draw_near_cols(key, part):
    key = jax.random.fold_in(key, 3)
    own_slot = (jnp.arange(NBT, dtype=jnp.int32) % PB)[:, None]
    others = jax.random.randint(key, (NBT, NEAR - 1), 0, NE).astype(jnp.int32)
    return jnp.concatenate([own_slot, others], axis=1)


def draw_near_blocks(key, part):
    key = jax.random.fold_in(key, 4)
    block_shape = (NBT, NEAR, BS, BS)
    noise = jnp.clip(jax.random.normal(key, block_shape, jnp.float32), -4.0, 4.0)
    first_entry = jnp.arange(NEAR) == 0
    spread = jnp.where(first_entry, 0.3, 0.6 / math.sqrt(NEAR - 1)) / math.sqrt(BS)
    leading = jnp.where(first_entry, 1.5, 0.0)
    identity = jnp.eye(BS, dtype=jnp.float32)
    return noise * spread[None, :, None, None] + leading[None, :, None, None] * identity


def draw_inverses(key, part):
    key = jax.random.fold_in(key, 6)
    noise_key, scale_key = jax.random.split(key)
    block_shape = (NBT // PB, NE, BS, BS)
    noise = jnp.clip(jax.random.normal(noise_key, block_shape, jnp.float32), -4.0, 4.0)
    diagonal = jax.random.uniform(scale_key, (NBT // PB, NE, 1, 1), jnp.float32, 0.4, 0.8)
    return diagonal * jnp.eye(BS, dtype=jnp.float32) + noise * (0.2 / math.sqrt(BS))


def draw_right_side(key, part):
    key = jax.random.fold_in(key, 5)
    value_key, scale_key = jax.random.split(key)
    position = (jnp.arange(NBT, dtype=jnp.float32) / NBT)[None, :, None]
    row_scale = jnp.exp(jax.random.uniform(scale_key, (1, NBT, 1), jnp.float32, 0.0, math.log(10.0)))
    values = jnp.clip(jax.random.normal(value_key, (NRHS, NBT, BS), jnp.float32), -5.0, 5.0)
    values = values * row_scale * (1.0 + 2.0 * position) / 4.0
    return values


def setup_inputs(seed: int = 0) -> dict:
    arg_keys = jax.random.split(jax.random.key(seed), 7)
    return {
        "right_side": draw_right_side(jax.random.fold_in(arg_keys[6], 71), 0),
        "patch_blocks": draw_patch_blocks(jax.random.fold_in(arg_keys[6], 71), 0),
        "send_rows": draw_send_rows(jax.random.fold_in(arg_keys[6], 71), 0),
        "near_cols": draw_near_cols(jax.random.fold_in(arg_keys[6], 71), 0),
        "near_blocks": draw_near_blocks(jax.random.fold_in(arg_keys[6], 71), 0),
        "inverses": draw_inverses(jax.random.fold_in(arg_keys[6], 71), 0),
    }


precise = lax.Precision.HIGHEST
epsilon = 1e-06

def least_squares(start_norm, lead_dot, lead_norm, upper_dot, lower_dot, tail_norm):
    radius_one = jnp.sqrt(lead_dot * lead_dot + lead_norm * lead_norm)
    cosine_one = lead_dot / radius_one
    sine_one = lead_norm / radius_one
    carried = cosine_one * upper_dot + sine_one * lower_dot
    rotated = cosine_one * lower_dot - sine_one * upper_dot
    radius_two = jnp.sqrt(rotated * rotated + tail_norm * tail_norm)
    coef_two = -start_norm * sine_one * rotated / (radius_two * radius_two)
    coef_one = (start_norm * cosine_one - carried * coef_two) / radius_one
    return (coef_one, coef_two)

def total_dot(first_field, second_field):
    return lax.optimization_barrier(jnp.sum(first_field * second_field, axis=(1, 2)))

def extend_all(vector, send_rows):
    patches = vector.reshape(NRHS, NBT // PB, PB, BS)
    from_prev = jnp.roll(patches, 1, axis=1)
    rows_prev = jnp.roll(send_rows[:, 0, :], 1, axis=0)
    from_next = jnp.roll(patches, -1, axis=1)
    rows_next = jnp.roll(send_rows[:, 1, :], -1, axis=0)
    full_shape = (NRHS, NBT // PB, NB, BS)
    picked_prev = jnp.take_along_axis(from_prev, jnp.broadcast_to(rows_prev[None, :, :, None], full_shape), axis=2)
    picked_next = jnp.take_along_axis(from_next, jnp.broadcast_to(rows_next[None, :, :, None], full_shape), axis=2)
    return jnp.concatenate([patches, picked_prev, picked_next], axis=2)

def near_product(extended, near_cols, near_blocks, live_mask):
    columns = near_cols.reshape(NBT // PB, PB, NEAR)
    blocks = near_blocks.reshape(NBT // PB, PB, NEAR, BS, BS)

    def one_patch(items):
        patch_ext, patch_cols, patch_blocks_near = items
        gathered = jnp.take(patch_ext, patch_cols, axis=1)
        return jnp.einsum('bkij,nbkj->nbi', patch_blocks_near, gathered, precision=precise)
    result = lax.map(one_patch, (jnp.moveaxis(extended, 1, 0), columns, blocks))
    return jnp.moveaxis(result, 0, 1).reshape(NRHS, NBT, BS) * live_mask

def reference(right_side, patch_blocks, send_rows, near_cols, near_blocks, inverses):
    slot_index = jnp.arange(PB, dtype=jnp.int32)
    live_mask = (slot_index[None, :] < patch_blocks[:, None]).astype(jnp.float32).reshape(1, NBT, 1)
    own_inverse = inverses[:, :PB].reshape(NBT, BS, BS)

    def operate(vector):
        return near_product(extend_all(vector, send_rows), near_cols, near_blocks, live_mask)

    def precondition(vector):
        extended = extend_all(vector, send_rows)
        smoothed = jnp.einsum('peij,npej->npei', inverses, extended, precision=precise)
        defect = vector - near_product(smoothed, near_cols, near_blocks, live_mask)
        own_smooth = smoothed[:, :, :PB].reshape(NRHS, NBT, BS)
        return (own_smooth + jnp.einsum('bij,nbj->nbi', own_inverse, defect, precision=precise)) * live_mask
    source = right_side * live_mask
    solution = jnp.zeros_like(source)
    for restart in range(CYCLES):
        if restart == 0:
            current = source
        else:
            current = source - operate(solution)
        start_norm = jnp.sqrt(total_dot(current, current) + epsilon)
        basis_first = current / start_norm[:, None, None]
        zeta_one = precondition(basis_first)
        mapped = operate(zeta_one)
        lead_dot = total_dot(mapped, basis_first)
        mapped = mapped - lead_dot[:, None, None] * basis_first
        lead_norm = jnp.sqrt(total_dot(mapped, mapped) + epsilon)
        basis_second = mapped / lead_norm[:, None, None]
        zeta_two = precondition(basis_second)
        mapped = operate(zeta_two)
        upper_dot = total_dot(mapped, basis_first)
        lower_dot = total_dot(mapped, basis_second)
        mapped = mapped - upper_dot[:, None, None] * basis_first
        mapped = mapped - lower_dot[:, None, None] * basis_second
        tail_norm = jnp.sqrt(total_dot(mapped, mapped) + epsilon)
        coef_one, coef_two = least_squares(start_norm, lead_dot, lead_norm, upper_dot, lower_dot, tail_norm)
        solution = solution + coef_one[:, None, None] * zeta_one + coef_two[:, None, None] * zeta_two
    return (solution, source - operate(solution))
```

```python
import functools

import jax
import jax.numpy as jnp
from jax import lax
from jax.experimental import pallas as pl
from jax.experimental.pallas import tpu as pltpu
from jax.sharding import PartitionSpec as P

CYCLES = 2
EPSILON = 1e-06
NB = 4
PB = 8
NE = 16
NEAR = 10
BS = 128
NRHS = 6
ROWS = 8
MESH = pl.DeviceIdType.MESH
F32 = jnp.float32
BF16 = jnp.bfloat16


def least_squares(start_norm, lead_dot, lead_norm, upper_dot, lower_dot, tail_norm):
    radius_one = jnp.sqrt(lead_dot * lead_dot + lead_norm * lead_norm)
    cosine_one = lead_dot / radius_one
    sine_one = lead_norm / radius_one
    carried = cosine_one * upper_dot + sine_one * lower_dot
    rotated = cosine_one * lower_dot - sine_one * upper_dot
    radius_two = jnp.sqrt(rotated * rotated + tail_norm * tail_norm)
    coef_two = -start_norm * sine_one * rotated / (radius_two * radius_two)
    coef_one = (start_norm * cosine_one - carried * coef_two) / radius_one
    return (coef_one, coef_two)


def split_three(value):
    high = value.astype(BF16).astype(F32)
    rest = value - high
    middle = rest.astype(BF16).astype(F32)
    return high, middle, rest - middle


def store_parts(ref, index, value):
    high, middle, low = split_three(value)
    ref[index, 0:16, :] = jnp.concatenate([high, middle], axis=0).astype(BF16)
    ref[index, 16:32, :] = jnp.concatenate([low, jnp.zeros_like(low)], axis=0).astype(BF16)


def store_matrix_parts(ref, index, rows, value):
    turned = value.T
    high = turned.astype(BF16)
    ref[index, rows, 0:BS] = high
    ref[index, rows, BS : 2 * BS] = (turned - high.astype(F32)).astype(BF16)


def product(parts, matrix):
    full = lax.dot_general(
        parts, matrix, (((1,), (0,)), ((), ())), preferred_element_type=F32
    )
    high, middle, low = full[0:8], full[8:16], full[16:24]
    smallest = low[:, 0:BS] + middle[:, BS : 2 * BS]
    return high[:, 0:BS] + (middle[:, 0:BS] + high[:, BS : 2 * BS] + smallest)


def kernel(
    shape,
    blocks_ref,
    rows_ref,
    cols_ref,
    right_ref,
    near_ref,
    inverse_ref,
    solution_ref,
    residual_ref,
    right_in,
    near_in,
    inverse_in,
    near_w,
    inverse_w,
    ext_parts,
    smooth_parts,
    smooth,
    defect_parts,
    field,
    picked,
    landed,
    dots,
    landed_dots,
    state,
    load_sem,
    swap_send,
    swap_recv,
    sum_send,
    sum_recv,
):
    size_x, size_z, size_y = shape
    patches = size_x * size_z * size_y
    patch = lax.axis_index("patch")
    core = lax.axis_index("grp")
    place_y = lax.rem(patch, size_y)
    place_z = lax.rem(lax.div(patch, size_y), size_z)
    place_x = lax.div(patch, size_y * size_z)
    before = lax.rem(patch + (patches - 1), patches)
    after = lax.rem(patch + 1, patches)
    other = 1 - core

    counts = (2 * size_z, size_x * size_y)

    def member(phase, offset):
        if phase == 0:
            place = lax.rem(place_z * 2 + core + offset, counts[0])
            spot_z, spot_core = lax.div(place, 2), lax.rem(place, 2)
            return ((place_x * size_z + spot_z) * size_y + place_y, spot_core)
        place = lax.rem(place_x * size_y + place_y + offset, counts[1])
        spot_x, spot_y = lax.div(place, size_y), lax.rem(place, size_y)
        return ((spot_x * size_z + place_z) * size_y + spot_y, core)

    barrier = pltpu.get_barrier_semaphore()
    greeted = 0
    for target in ((patch, other), (before, core), (before, other), (after, core), (after, other)):
        pl.semaphore_signal(barrier, inc=1, device_id=target, device_id_type=MESH)
        greeted += 1
    for phase in range(2):
        for offset in range(1, counts[phase]):
            pl.semaphore_signal(
                barrier, inc=1, device_id=member(phase, offset), device_id_type=MESH
            )
            greeted += 1

    loads = [pltpu.make_async_copy(right_ref, right_in, load_sem.at[0])]
    loads += [pltpu.make_async_copy(inverse_ref.at[0], inverse_in, load_sem.at[1])]
    loads += [
        pltpu.make_async_copy(near_ref.at[b], near_in.at[b], load_sem.at[2 + b])
        for b in range(NB)
    ]
    for load in loads:
        load.start()

    first_slot = core * NB
    live = [
        jnp.where(first_slot + s < blocks_ref[0], jnp.float32(1), jnp.float32(0))
        for s in range(NB)
    ]
    lane = lax.broadcasted_iota(jnp.int32, (ROWS, BS), 1)

    def swap_copies(kind):
        own, to_after, to_before = field.at[kind], picked.at[kind, 0], picked.at[kind, 1]
        plan = (
            (to_after, 1, (after, core)),
            (to_after, 2, (after, other)),
            (to_before, 3, (before, core)),
            (to_before, 4, (before, other)),
            (own, 0, (patch, other)),
        )
        return [
            pltpu.make_async_remote_copy(
                src_ref=source,
                dst_ref=landed.at[kind, slot],
                send_sem=swap_send.at[kind, slot],
                recv_sem=swap_recv.at[kind, slot],
                device_id=target,
                device_id_type=MESH,
            )
            for source, slot, target in plan
        ]

    def start_swap(kind):
        for way in range(2):
            for o in range(NB):
                row = rows_ref[0, way, o]
                mine = jnp.where(
                    jnp.logical_and(row >= first_slot, row < first_slot + NB),
                    jnp.float32(1),
                    jnp.float32(0),
                )
                picked[kind, way, o] = field[kind, jnp.bitwise_and(row, NB - 1)] * mine
        copies = swap_copies(kind)
        for copy in copies:
            copy.start()
        return copies

    def sum_copies(parity, phase):
        return [
            pltpu.make_async_remote_copy(
                src_ref=dots.at[parity, phase],
                dst_ref=landed_dots.at[parity, phase, offset],
                send_sem=sum_send.at[parity, phase, offset],
                recv_sem=sum_recv.at[parity, phase, offset],
                device_id=member(phase, offset),
                device_id_type=MESH,
            )
            for offset in range(1, counts[phase])
        ]

    def start_sum(parity, phase):
        copies = sum_copies(parity, phase)
        for copy in copies:
            copy.start()
        return copies

    def finish_sum(copies, parity, phase):
        total = dots[parity, phase]
        for offset, copy in enumerate(copies, 1):
            copy.wait_recv()
            total = total + landed_dots[parity, phase, offset]
        for copy in copies:
            copy.wait_send()
        return total

    def extend(kind, copies, then):
        for s in range(NB):
            store_parts(ext_parts, first_slot + s, field[kind, s])
            then(first_slot + s)
        copies[4].wait_recv()
        for s in range(NB):
            store_parts(ext_parts, other * NB + s, landed[kind, 0, s])
            then(other * NB + s)
        for way in range(2):
            copies[2 * way].wait_recv()
            copies[1 + 2 * way].wait_recv()
            for o in range(NB):
                value = landed[kind, 1 + 2 * way, o] + landed[kind, 2 + 2 * way, o]
                store_parts(ext_parts, PB + NB * way + o, value)
                then(PB + NB * way + o)

    def near_product(parts_ref, b):
        gathered = jnp.concatenate([parts_ref[cols_ref[b, k]] for k in range(NEAR)], axis=1)
        return product(gathered, near_w[b])

    def smooth_block(e):
        value = product(ext_parts[e], inverse_w[e])
        smooth[e] = value
        store_parts(smooth_parts, e, value)

    def precondition(copies):
        extend(0, copies, smooth_block)
        for b in range(NB):
            defect = field[0, b] - near_product(smooth_parts, b)
            store_parts(defect_parts, b, defect)
        for b in range(NB):
            inner = product(defect_parts[b], inverse_w[first_slot + b])
            field[1, b] = (smooth[first_slot + b] + inner) * live[b]

    def dot_tile(pairs):
        tile = jnp.zeros((ROWS, BS), F32)
        for q, (left, right) in enumerate(pairs):
            partial = left[0] * right[0]
            for s in range(1, NB):
                partial = partial + left[s] * right[s]
            total = jnp.sum(partial, axis=1, keepdims=True)
            tile = jnp.where(lane == q, total, tile)
        return tile

    def pick(tile, q):
        return jnp.broadcast_to(tile[:, q : q + 1], (ROWS, BS))

    loads[0].wait()
    empty = jnp.zeros((ROWS - NRHS, BS), F32)
    for s in range(NB):
        value = jnp.concatenate([right_in[:, s, :], empty], axis=0) * live[s]
        field[0, s] = value
        state[0, s] = value
    source = [state[0, s] for s in range(NB)]
    dots[0, 0] = dot_tile([(source, source)])

    pl.semaphore_wait(barrier, greeted)
    first_copies = start_swap(0)
    loads[1].wait()
    for e in range(NE):
        store_matrix_parts(inverse_w, e, slice(0, BS), inverse_in[e])
    for b in range(NB):
        loads[2 + b].wait()
        for k in range(NEAR):
            store_matrix_parts(near_w, b, slice(k * BS, (k + 1) * BS), near_in[b, k])

    R, FIRST, ZETA1, MAPPED1, SECOND, ZETA2, MAPPED2, RAWZ, RAWM, SOL = range(10)

    def get(index):
        return [state[index, s] for s in range(NB)]

    def put(index, values):
        for s in range(NB):
            state[index, s] = values[s]

    def combine(*terms):
        out = []
        for s in range(NB):
            value = None
            for coefficient, vector in terms:
                term = vector[s] if coefficient is None else coefficient * vector[s]
                value = term if value is None else value + term
            out.append(value)
        return out

    def begin(total):
        square = pick(total, 0)
        norm = jnp.sqrt(square + EPSILON)
        return norm, square / (norm * norm)

    def extend_basis(lead_dot, lead_square, first_square):
        reduced = lead_square - lead_dot * lead_dot * (2.0 - first_square)
        return jnp.sqrt(jnp.maximum(reduced, 0.0) + EPSILON)

    def second_dots(first, second, mapped):
        return dot_tile(
            [(mapped, first), (mapped, second), (mapped, mapped), (first, second), (second, second)]
        )

    def coefficients(total, norm, first_square, lead_dot, lead_norm):
        upper, lower, square, cross, second_square = [pick(total, q) for q in range(5)]
        tail = (
            square
            - upper * upper * (2.0 - first_square)
            - lower * lower * (2.0 - second_square)
            + 2.0 * upper * lower * cross
        )
        tail_norm = jnp.sqrt(jnp.maximum(tail, 0.0) + EPSILON)
        return least_squares(norm, lead_dot, lead_norm, upper, lower, tail_norm)

    zero = jnp.zeros((ROWS, BS), F32)

    def step(i, carry):
        norm, first_square, lead_dot, lead_norm = carry
        parity = lax.rem(i, 2)
        copies = swap_copies(0)
        partial = start_sum(parity, 0)
        precondition(copies)
        for copy in copies:
            copy.wait_send()
        copies = start_swap(1)
        dots[parity, 1] = finish_sum(partial, parity, 0)
        partial = start_sum(parity, 1)
        extend(1, copies, lambda e: None)
        for copy in copies:
            copy.wait_send()
        for b in range(NB):
            field[0, b] = near_product(ext_parts, b) * live[b]
        total = finish_sum(partial, parity, 1)
        return total, norm, first_square, lead_dot, lead_norm

    def zetas():
        return [field[1, s] for s in range(NB)], [field[0, s] for s in range(NB)]

    def advance(i, values):
        for s in range(NB):
            field[0, s] = values[s]
        return start_swap(0)

    def body(i, carry):
        total, norm, first_square, lead_dot, lead_norm = step(i, carry)
        following = 1 - lax.rem(i, 2)
        zeta, mapped = zetas()

        @pl.when(i == 0)
        def _():
            norm_now, _ = begin(total)
            scale = 1.0 / norm_now
            first = combine((scale, get(R)))
            mapped_one = combine((scale, mapped))
            advance(i, mapped_one)
            put(FIRST, first)
            put(ZETA1, combine((scale, zeta)))
            put(MAPPED1, mapped_one)
            dots[following, 0] = dot_tile([(mapped_one, first), (mapped_one, mapped_one)])

        norm_now, square_now = begin(total)
        norm = jnp.where(i == 0, norm_now, norm)
        first_square = jnp.where(i == 0, square_now, first_square)

        lead_now = pick(total, 0)
        lead_norm_now = extend_basis(lead_now, pick(total, 1), first_square)
        lead_dot = jnp.where(i == 1, lead_now, lead_dot)
        lead_norm = jnp.where(i == 1, lead_norm_now, lead_norm)

        @pl.when(i == 1)
        def _():
            scale = 1.0 / lead_norm
            first, zeta_one, mapped_one = get(FIRST), get(ZETA1), get(MAPPED1)
            mapped_two = combine((scale, combine((None, mapped), (-lead_dot, mapped_one))))
            advance(i, mapped_two)
            second = combine((scale, combine((None, mapped_one), (-lead_dot, first))))
            put(RAWZ, zeta)
            put(RAWM, mapped)
            put(ZETA2, combine((scale, combine((None, zeta), (-lead_dot, zeta_one)))))
            put(MAPPED2, mapped_two)
            dots[following, 0] = second_dots(first, second, mapped_two)

        @pl.when(i == 2)
        def _():
            one, two = coefficients(total, norm, first_square, lead_dot, lead_norm)
            mapped_one, mapped_two, zeta_one = get(MAPPED1), get(MAPPED2), get(ZETA1)
            mapped_next = combine((norm, mapped_one), (-one, get(RAWM)), (-two, mapped))
            advance(i, mapped_next)
            current = combine((None, get(R)), (-one, mapped_one), (-two, mapped_two))
            put(SOL, combine((one, zeta_one), (two, get(ZETA2))))
            put(ZETA1, combine((norm, zeta_one), (-one, get(RAWZ)), (-two, zeta)))
            put(MAPPED1, mapped_next)
            put(R, current)
            dots[following, 0] = dot_tile(
                [(current, current), (current, mapped_next), (mapped_next, mapped_next)]
            )

        return total, norm, first_square, lead_dot, lead_norm

    state_now = (zero, zero, zero, zero)
    carry = (zero,) + state_now

    def loop_body(i, carry):
        return body(i, carry[1:])

    carry = lax.fori_loop(0, 3, loop_body, carry)
    total = step(3, carry[1:])[0]
    zeta, mapped = zetas()
    norm, first_square = begin(total)
    inverse_norm = 1.0 / norm
    current = get(R)
    first = combine((inverse_norm, current))
    mapped_one = combine((inverse_norm, get(MAPPED1)))
    zeta_one = combine((inverse_norm, get(ZETA1)))
    lead_dot = pick(total, 1) * inverse_norm * inverse_norm
    lead_norm = extend_basis(
        lead_dot, pick(total, 2) * inverse_norm * inverse_norm, first_square
    )
    scale = 1.0 / lead_norm
    second = combine((scale, combine((None, mapped_one), (-lead_dot, first))))
    mapped_two = combine((scale, combine((inverse_norm, mapped), (-lead_dot, mapped_one))))
    dots[0, 0] = second_dots(first, second, mapped_two)
    partial = start_sum(0, 0)
    zeta_two = combine((scale, combine((inverse_norm, zeta), (-lead_dot, zeta_one))))
    dots[0, 1] = finish_sum(partial, 0, 0)
    total = finish_sum(start_sum(0, 1), 0, 1)
    one, two = coefficients(total, norm, first_square, lead_dot, lead_norm)
    answer = combine((None, get(SOL)), (one, zeta_one), (two, zeta_two))
    left = combine((None, current), (-one, mapped_one), (-two, mapped_two))
    for s in range(NB):
        solution_ref[:, s, :] = answer[s][0:NRHS]
        residual_ref[:, s, :] = left[s][0:NRHS]


def factors(patches):
    known = {128: (4, 8, 4), 8: (2, 2, 2), 4: (1, 2, 2)}
    return known.get(patches, (1, patches, 1))


def local(shape, right_side, patch_blocks, send_rows, near_cols, near_blocks, inverses):
    counts = (2 * shape[1], shape[0] * shape[2])
    most = max(counts)
    field = jax.ShapeDtypeStruct(right_side.shape, F32)
    smem = pl.BlockSpec(memory_space=pltpu.SMEM)
    vmem = pl.BlockSpec(memory_space=pltpu.VMEM)
    anywhere = pl.BlockSpec(memory_space=pl.ANY)
    return pl.pallas_call(
        functools.partial(kernel, shape),
        out_shape=(field, field),
        in_specs=[smem, smem, smem, anywhere, anywhere, anywhere],
        out_specs=(vmem, vmem),
        scratch_shapes=[
            pltpu.VMEM((NRHS, NB, BS), F32),
            pltpu.VMEM((NB, NEAR, BS, BS), F32),
            pltpu.VMEM((NE, BS, BS), F32),
            pltpu.VMEM((NB, NEAR * BS, 2 * BS), BF16),
            pltpu.VMEM((NE, BS, 2 * BS), BF16),
            pltpu.VMEM((NE, 32, BS), BF16),
            pltpu.VMEM((NE, 32, BS), BF16),
            pltpu.VMEM((NE, ROWS, BS), F32),
            pltpu.VMEM((NB, 32, BS), BF16),
            pltpu.VMEM((2, NB, ROWS, BS), F32),
            pltpu.VMEM((2, 2, NB, ROWS, BS), F32),
            pltpu.VMEM((2, 5, NB, ROWS, BS), F32),
            pltpu.VMEM((2, 2, ROWS, BS), F32),
            pltpu.VMEM((2, 2, most, ROWS, BS), F32),
            pltpu.VMEM((10, NB, ROWS, BS), F32),
            pltpu.SemaphoreType.DMA((2 + NB,)),
            pltpu.SemaphoreType.DMA((2, 5)),
            pltpu.SemaphoreType.DMA((2, 5)),
            pltpu.SemaphoreType.DMA((2, 2, most)),
            pltpu.SemaphoreType.DMA((2, 2, most)),
        ],
        compiler_params=pltpu.CompilerParams(
            collective_id=0, has_side_effects=True, vmem_limit_bytes=60 * 1024 * 1024
        ),
        name="gmres",
    )(patch_blocks, send_rows, near_cols, right_side, near_blocks, inverses)


def solution(mesh):
    in_specs = (
        P(None, ("patch", "grp"), None),
        P("patch"),
        P("patch", None, None),
        P(("patch", "grp"), None),
        P(("patch", "grp"), None, None, None),
        P("patch", None, None, None),
    )
    out_specs = (P(None, ("patch", "grp"), None), P(None, ("patch", "grp"), None))
    shape = factors(mesh.shape["patch"])
    return jax.shard_map(
        functools.partial(local, shape),
        mesh=mesh,
        in_specs=in_specs,
        out_specs=out_specs,
        check_vma=False,
    )
```

```python
import functools

import jax
import jax.numpy as jnp
from jax import lax
from jax.experimental import pallas as pl
from jax.experimental.pallas import tpu as pltpu
from jax.sharding import PartitionSpec as P

CYCLES = 2
EPSILON = 1e-06
NB = 4
PB = 8
NE = 16
NEAR = 10
BS = 128
NRHS = 6
ROWS = 8
MESH = pl.DeviceIdType.MESH
F32 = jnp.float32
BF16 = jnp.bfloat16


def least_squares(start_norm, lead_dot, lead_norm, upper_dot, lower_dot, tail_norm):
    radius_one = jnp.sqrt(lead_dot * lead_dot + lead_norm * lead_norm)
    cosine_one = lead_dot / radius_one
    sine_one = lead_norm / radius_one
    carried = cosine_one * upper_dot + sine_one * lower_dot
    rotated = cosine_one * lower_dot - sine_one * upper_dot
    radius_two = jnp.sqrt(rotated * rotated + tail_norm * tail_norm)
    coef_two = -start_norm * sine_one * rotated / (radius_two * radius_two)
    coef_one = (start_norm * cosine_one - carried * coef_two) / radius_one
    return (coef_one, coef_two)


def split_three(value):
    high = value.astype(BF16).astype(F32)
    rest = value - high
    middle = rest.astype(BF16).astype(F32)
    return high, middle, rest - middle


def store_parts(ref, index, value):
    high, middle, low = split_three(value)
    ref[index, 0:16, :] = jnp.concatenate([high, middle], axis=0).astype(BF16)
    ref[index, 16:32, :] = jnp.concatenate([low, jnp.zeros_like(low)], axis=0).astype(BF16)


def matrix_parts(value, axis):
    high = value.astype(BF16)
    return jnp.concatenate([high, (value - high.astype(F32)).astype(BF16)], axis=axis)


def matrix_product(left, right):
    full = jnp.dot(left, right, preferred_element_type=F32)
    cross = full[0:BS, BS : 2 * BS] + full[BS : 2 * BS, 0:BS] + full[BS : 2 * BS, BS : 2 * BS]
    return full[0:BS, 0:BS] + cross


def product(parts, matrix):
    full = lax.dot_general(
        parts, matrix, (((1,), (0,)), ((), ())), preferred_element_type=F32
    )
    high, middle, low = full[0:8], full[8:16], full[16:24]
    smallest = low[:, 0:BS] + middle[:, BS : 2 * BS]
    return high[:, 0:BS] + (middle[:, 0:BS] + high[:, BS : 2 * BS] + smallest)


def kernel(
    shape,
    blocks_ref,
    rows_hbm,
    cols_hbm,
    right_ref,
    near_ref,
    inverse_ref,
    both_ref,
    rows_ref,
    cols_ref,
    right_in,
    near_in,
    inverse_in,
    near_w,
    mixed_w,
    inverse_parts,
    ext_parts,
    field,
    picked,
    landed,
    dots,
    landed_dots,
    state,
    load_sem,
    swap_send,
    swap_recv,
    sum_send,
    sum_recv,
):
    size_x, size_z, size_y = shape
    patches = size_x * size_z * size_y
    patch = lax.axis_index("patch")
    core = lax.axis_index("grp")
    place_y = lax.rem(patch, size_y)
    place_z = lax.rem(lax.div(patch, size_y), size_z)
    place_x = lax.div(patch, size_y * size_z)
    before = lax.rem(patch + (patches - 1), patches)
    after = lax.rem(patch + 1, patches)
    other = 1 - core

    counts = (2 * size_z, size_x * size_y)

    def member(phase, offset):
        if phase == 0:
            place = lax.rem(place_z * 2 + core + offset, counts[0])
            spot_z, spot_core = lax.div(place, 2), lax.rem(place, 2)
            return ((place_x * size_z + spot_z) * size_y + place_y, spot_core)
        place = lax.rem(place_x * size_y + place_y + offset, counts[1])
        spot_x, spot_y = lax.div(place, size_y), lax.rem(place, size_y)
        return ((spot_x * size_z + place_z) * size_y + spot_y, core)

    barrier = pltpu.get_barrier_semaphore()
    greeted = 0
    for target in ((patch, other), (before, core), (before, other), (after, core), (after, other)):
        pl.semaphore_signal(barrier, inc=1, device_id=target, device_id_type=MESH)
        greeted += 1
    for phase in range(2):
        for offset in range(1, counts[phase]):
            pl.semaphore_signal(
                barrier, inc=1, device_id=member(phase, offset), device_id_type=MESH
            )
            greeted += 1

    loads = [pltpu.make_async_copy(right_ref, right_in, load_sem.at[0])]
    loads += [pltpu.make_async_copy(inverse_ref.at[0], inverse_in, load_sem.at[1])]
    loads += [
        pltpu.make_async_copy(near_ref.at[b], near_in.at[b], load_sem.at[2 + b])
        for b in range(NB)
    ]
    loads += [
        pltpu.make_async_copy(source, target, load_sem.at[2 + NB + i])
        for i, (source, target) in enumerate(((rows_hbm, rows_ref), (cols_hbm, cols_ref)))
    ]
    for load in loads[2 + NB :] + loads[: 2 + NB]:
        load.start()
    for load in loads[2 + NB :]:
        load.wait()

    first_slot = core * NB
    live = [
        jnp.where(first_slot + s < blocks_ref[0], jnp.float32(1), jnp.float32(0))
        for s in range(NB)
    ]
    lane = lax.broadcasted_iota(jnp.int32, (ROWS, BS), 1)
    case = lax.broadcasted_iota(jnp.int32, (ROWS, BS), 0)

    def swap_copies(kind):
        own, to_after, to_before = field.at[kind], picked.at[kind, 0], picked.at[kind, 1]
        plan = (
            (to_after, 1, (after, core)),
            (to_after, 2, (after, other)),
            (to_before, 3, (before, core)),
            (to_before, 4, (before, other)),
            (own, 0, (patch, other)),
        )
        return [
            pltpu.make_async_remote_copy(
                src_ref=source,
                dst_ref=landed.at[kind, slot],
                send_sem=swap_send.at[kind, slot],
                recv_sem=swap_recv.at[kind, slot],
                device_id=target,
                device_id_type=MESH,
            )
            for source, slot, target in plan
        ]

    def start_swap(kind):
        for way in range(2):
            for o in range(NB):
                row = rows_ref[0, way, o]
                mine = jnp.where(
                    jnp.logical_and(row >= first_slot, row < first_slot + NB),
                    jnp.float32(1),
                    jnp.float32(0),
                )
                picked[kind, way, o] = field[kind, jnp.bitwise_and(row, NB - 1)] * mine
        copies = swap_copies(kind)
        for copy in copies:
            copy.start()
        return copies

    def sum_copies(parity, phase):
        return [
            pltpu.make_async_remote_copy(
                src_ref=dots.at[parity, phase],
                dst_ref=landed_dots.at[parity, phase, offset],
                send_sem=sum_send.at[parity, phase, offset],
                recv_sem=sum_recv.at[parity, phase, offset],
                device_id=member(phase, offset),
                device_id_type=MESH,
            )
            for offset in range(1, counts[phase])
        ]

    def start_sum(parity, phase):
        copies = sum_copies(parity, phase)
        for copy in copies:
            copy.start()
        return copies

    def finish_sum(copies, parity, phase):
        total = dots[parity, phase]
        for offset, copy in enumerate(copies, 1):
            copy.wait_recv()
            total = total + landed_dots[parity, phase, offset]
        for copy in copies:
            copy.wait_send()
        return total

    def extend(kind, copies):
        for s in range(NB):
            store_parts(ext_parts, first_slot + s, field[kind, s])
        copies[4].wait_recv()
        for s in range(NB):
            store_parts(ext_parts, other * NB + s, landed[kind, 0, s])
        for way in range(2):
            copies[2 * way].wait_recv()
            copies[1 + 2 * way].wait_recv()
            for o in range(NB):
                value = landed[kind, 1 + 2 * way, o] + landed[kind, 2 + 2 * way, o]
                store_parts(ext_parts, PB + NB * way + o, value)

    def apply_blocks(weights, b):
        gathered = jnp.concatenate([ext_parts[cols_ref[b, k]] for k in range(NEAR)], axis=1)
        return product(gathered, weights[b]) * live[b]

    def dot_tile(pairs):
        tile = jnp.zeros((ROWS, BS), F32)
        for q, (left, right) in enumerate(pairs):
            partial = left[0] * right[0]
            for s in range(1, NB):
                partial = partial + left[s] * right[s]
            total = jnp.sum(partial, axis=1, keepdims=True)
            tile = jnp.where(lane == q * ROWS + case, total, tile)
        return jnp.sum(tile, axis=0, keepdims=True)

    def pick(tile, q):
        mine = jnp.where(lane == q * ROWS + case, jnp.broadcast_to(tile, (ROWS, BS)), 0.0)
        return jnp.broadcast_to(jnp.sum(mine, axis=1, keepdims=True), (ROWS, BS))

    loads[0].wait()
    empty = jnp.zeros((ROWS - NRHS, BS), F32)
    for s in range(NB):
        value = jnp.concatenate([right_in[:, s, :], empty], axis=0) * live[s]
        field[0, s] = value
        state[0, s] = value
    source = [state[0, s] for s in range(NB)]
    dots[0, 0] = dot_tile([(source, source)])

    pl.semaphore_wait(barrier, greeted)
    first_copies = start_swap(0)
    loads[1].wait()
    for e in range(NE):
        inverse_parts[e] = matrix_parts(inverse_in[e], 1)

    @pl.loop(0, NB)
    def _(b):
        pltpu.make_async_copy(near_ref.at[b], near_in.at[b], load_sem.at[2 + b]).wait()
        own = inverse_in[first_slot + b]
        own_parts = matrix_parts(own, 0)
        for k in range(NEAR):
            rows = slice(k * BS, (k + 1) * BS)
            block = near_in[b, k]
            left = matrix_product(own_parts, matrix_parts(block, 1))
            value = -matrix_product(matrix_parts(left, 0), inverse_parts[cols_ref[b, k]])
            if k == 0:
                value = 2.0 * own + value
            mixed_w[b, rows, :] = matrix_parts(value.T, 1)
            near_w[b, rows, :] = matrix_parts(block.T, 1)

    R, FIRST, ZETA1, MAPPED1, SECOND, ZETA2, MAPPED2, RAWZ, RAWM, SOL = range(10)

    def get(index):
        return [state[index, s] for s in range(NB)]

    def put(index, values):
        for s in range(NB):
            state[index, s] = values[s]

    def combine(*terms):
        out = []
        for s in range(NB):
            value = None
            for coefficient, vector in terms:
                term = vector[s] if coefficient is None else coefficient * vector[s]
                value = term if value is None else value + term
            out.append(value)
        return out

    def begin(total):
        square = pick(total, 0)
        norm = jnp.sqrt(square + EPSILON)
        return norm, square / (norm * norm)

    def extend_basis(lead_dot, lead_square, first_square):
        reduced = lead_square - lead_dot * lead_dot * (2.0 - first_square)
        return jnp.sqrt(jnp.maximum(reduced, 0.0) + EPSILON)

    def second_dots(first, second, mapped):
        return dot_tile(
            [(mapped, first), (mapped, second), (mapped, mapped), (first, second), (second, second)]
        )

    def coefficients(total, norm, first_square, lead_dot, lead_norm):
        upper, lower, square, cross, second_square = [pick(total, q) for q in range(5)]
        tail = (
            square
            - upper * upper * (2.0 - first_square)
            - lower * lower * (2.0 - second_square)
            + 2.0 * upper * lower * cross
        )
        tail_norm = jnp.sqrt(jnp.maximum(tail, 0.0) + EPSILON)
        return least_squares(norm, lead_dot, lead_norm, upper, lower, tail_norm)

    zero = jnp.zeros((ROWS, BS), F32)

    def step(i, carry):
        norm, first_square, lead_dot, lead_norm = carry
        parity = lax.rem(i, 2)
        copies = swap_copies(0)
        partial = start_sum(parity, 0)
        extend(0, copies)
        for b in range(NB):
            field[1, b] = apply_blocks(mixed_w, b)
        for copy in copies:
            copy.wait_send()
        copies = start_swap(1)
        dots[parity, 1] = finish_sum(partial, parity, 0)
        partial = start_sum(parity, 1)
        extend(1, copies)
        for copy in copies:
            copy.wait_send()
        for b in range(NB):
            field[0, b] = apply_blocks(near_w, b)
        total = finish_sum(partial, parity, 1)
        return total, norm, first_square, lead_dot, lead_norm

    def zetas():
        return [field[1, s] for s in range(NB)], [field[0, s] for s in range(NB)]

    def advance(i, values):
        for s in range(NB):
            field[0, s] = values[s]
        return start_swap(0)

    def body(i, carry):
        total, norm, first_square, lead_dot, lead_norm = step(i, carry)
        following = 1 - lax.rem(i, 2)
        zeta, mapped = zetas()

        @pl.when(i == 0)
        def _():
            norm_now, _ = begin(total)
            scale = 1.0 / norm_now
            first = combine((scale, get(R)))
            mapped_one = combine((scale, mapped))
            advance(i, mapped_one)
            put(FIRST, first)
            put(ZETA1, combine((scale, zeta)))
            put(MAPPED1, mapped_one)
            dots[following, 0] = dot_tile([(mapped_one, first), (mapped_one, mapped_one)])

        norm_now, square_now = begin(total)
        norm = jnp.where(i == 0, norm_now, norm)
        first_square = jnp.where(i == 0, square_now, first_square)

        lead_now = pick(total, 0)
        lead_norm_now = extend_basis(lead_now, pick(total, 1), first_square)
        lead_dot = jnp.where(i == 1, lead_now, lead_dot)
        lead_norm = jnp.where(i == 1, lead_norm_now, lead_norm)

        @pl.when(i == 1)
        def _():
            scale = 1.0 / lead_norm
            first, zeta_one, mapped_one = get(FIRST), get(ZETA1), get(MAPPED1)
            mapped_two = combine((scale, combine((None, mapped), (-lead_dot, mapped_one))))
            advance(i, mapped_two)
            second = combine((scale, combine((None, mapped_one), (-lead_dot, first))))
            put(RAWZ, zeta)
            put(RAWM, mapped)
            put(ZETA2, combine((scale, combine((None, zeta), (-lead_dot, zeta_one)))))
            put(MAPPED2, mapped_two)
            dots[following, 0] = second_dots(first, second, mapped_two)

        @pl.when(i == 2)
        def _():
            one, two = coefficients(total, norm, first_square, lead_dot, lead_norm)
            mapped_one, mapped_two, zeta_one = get(MAPPED1), get(MAPPED2), get(ZETA1)
            mapped_next = combine((norm, mapped_one), (-one, get(RAWM)), (-two, mapped))
            advance(i, mapped_next)
            current = combine((None, get(R)), (-one, mapped_one), (-two, mapped_two))
            put(SOL, combine((one, zeta_one), (two, get(ZETA2))))
            put(ZETA1, combine((norm, zeta_one), (-one, get(RAWZ)), (-two, zeta)))
            put(MAPPED1, mapped_next)
            put(R, current)
            dots[following, 0] = dot_tile(
                [(current, current), (current, mapped_next), (mapped_next, mapped_next)]
            )

        return total, norm, first_square, lead_dot, lead_norm

    state_now = (zero, zero, zero, zero)
    carry = (jnp.zeros((1, BS), F32),) + state_now

    def loop_body(i, carry):
        return body(i, carry[1:])

    carry = lax.fori_loop(0, 3, loop_body, carry)
    total = step(3, carry[1:])[0]
    zeta, mapped = zetas()
    norm, first_square = begin(total)
    inverse_norm = 1.0 / norm
    current = get(R)
    first = combine((inverse_norm, current))
    mapped_one = combine((inverse_norm, get(MAPPED1)))
    zeta_one = combine((inverse_norm, get(ZETA1)))
    lead_dot = pick(total, 1) * inverse_norm * inverse_norm
    lead_norm = extend_basis(
        lead_dot, pick(total, 2) * inverse_norm * inverse_norm, first_square
    )
    scale = 1.0 / lead_norm
    second = combine((scale, combine((None, mapped_one), (-lead_dot, first))))
    mapped_two = combine((scale, combine((inverse_norm, mapped), (-lead_dot, mapped_one))))
    dots[0, 0] = second_dots(first, second, mapped_two)
    partial = start_sum(0, 0)
    zeta_two = combine((scale, combine((inverse_norm, zeta), (-lead_dot, zeta_one))))
    dots[0, 1] = finish_sum(partial, 0, 0)
    total = finish_sum(start_sum(0, 1), 0, 1)
    one, two = coefficients(total, norm, first_square, lead_dot, lead_norm)
    answer = combine((None, get(SOL)), (one, zeta_one), (two, zeta_two))
    left = combine((None, current), (-one, mapped_one), (-two, mapped_two))
    for s in range(NB):
        both_ref[0, :, s, :] = answer[s][0:NRHS]
        both_ref[1, :, s, :] = left[s][0:NRHS]


def factors(patches):
    known = {128: (4, 8, 4), 8: (2, 2, 2), 4: (1, 2, 2)}
    return known.get(patches, (1, patches, 1))


def local(shape, right_side, patch_blocks, send_rows, near_cols, near_blocks, inverses):
    counts = (2 * shape[1], shape[0] * shape[2])
    most = max(counts)
    field = jax.ShapeDtypeStruct((2,) + right_side.shape, F32)
    vmem = pl.BlockSpec(memory_space=pltpu.VMEM)
    hbm = pl.BlockSpec(memory_space=pltpu.HBM)
    send_rows, near_cols, right_side, near_blocks, inverses = [
        pltpu.with_memory_space_constraint(value, pltpu.HBM)
        for value in (send_rows, near_cols, right_side, near_blocks, inverses)
    ]
    both = pl.pallas_call(
        functools.partial(kernel, shape),
        out_shape=field,
        in_specs=[pl.BlockSpec(memory_space=pltpu.SMEM)] + [hbm] * 5,
        out_specs=vmem,
        scratch_shapes=[
            pltpu.SMEM((1, 2, NB), jnp.int32),
            pltpu.SMEM((NB, NEAR), jnp.int32),
            pltpu.VMEM((NRHS, NB, BS), F32),
            pltpu.VMEM((NB, NEAR, BS, BS), F32),
            pltpu.VMEM((NE, BS, BS), F32),
            pltpu.VMEM((NB, NEAR * BS, 2 * BS), BF16),
            pltpu.VMEM((NB, NEAR * BS, 2 * BS), BF16),
            pltpu.VMEM((NE, BS, 2 * BS), BF16),
            pltpu.VMEM((NE, 32, BS), BF16),
            pltpu.VMEM((2, NB, ROWS, BS), F32),
            pltpu.VMEM((2, 2, NB, ROWS, BS), F32),
            pltpu.VMEM((2, 5, NB, ROWS, BS), F32),
            pltpu.VMEM((2, 2, 1, BS), F32),
            pltpu.VMEM((2, 2, most, 1, BS), F32),
            pltpu.VMEM((10, NB, ROWS, BS), F32),
            pltpu.SemaphoreType.DMA((4 + NB,)),
            pltpu.SemaphoreType.DMA((2, 5)),
            pltpu.SemaphoreType.DMA((2, 5)),
            pltpu.SemaphoreType.DMA((2, 2, most)),
            pltpu.SemaphoreType.DMA((2, 2, most)),
        ],
        compiler_params=pltpu.CompilerParams(
            collective_id=0, has_side_effects=True, vmem_limit_bytes=32 * 1024 * 1024
        ),
        name="gmres",
    )(patch_blocks, send_rows, near_cols, right_side, near_blocks, inverses)
    return both[0], both[1]


def solution(mesh):
    in_specs = (
        P(None, ("patch", "grp"), None),
        P("patch"),
        P("patch", None, None),
        P(("patch", "grp"), None),
        P(("patch", "grp"), None, None, None),
        P("patch", None, None, None),
    )
    out_specs = (P(None, ("patch", "grp"), None), P(None, ("patch", "grp"), None))
    shape = factors(mesh.shape["patch"])
    return jax.shard_map(
        functools.partial(local, shape),
        mesh=mesh,
        in_specs=in_specs,
        out_specs=out_specs,
        check_vma=False,
    )
```

```python
import functools

import jax
import jax.numpy as jnp
from jax import lax
from jax.experimental import pallas as pl
from jax.experimental.pallas import tpu as pltpu
from jax.sharding import PartitionSpec as P

CYCLES = 2
EPSILON = 1e-06
NB = 4
PB = 8
NE = 16
NEAR = 10
BS = 128
NRHS = 6
ROWS = 8
MESH = pl.DeviceIdType.MESH
F32 = jnp.float32
BF16 = jnp.bfloat16


def least_squares(start_norm, lead_dot, lead_norm, upper_dot, lower_dot, tail_norm):
    radius_one = jnp.sqrt(lead_dot * lead_dot + lead_norm * lead_norm)
    cosine_one = lead_dot / radius_one
    sine_one = lead_norm / radius_one
    carried = cosine_one * upper_dot + sine_one * lower_dot
    rotated = cosine_one * lower_dot - sine_one * upper_dot
    radius_two = jnp.sqrt(rotated * rotated + tail_norm * tail_norm)
    coef_two = -start_norm * sine_one * rotated / (radius_two * radius_two)
    coef_one = (start_norm * cosine_one - carried * coef_two) / radius_one
    return (coef_one, coef_two)


def split_three(value):
    high = value.astype(BF16).astype(F32)
    rest = value - high
    middle = rest.astype(BF16).astype(F32)
    return high, middle, rest - middle


def store_parts(ref, index, value):
    high, middle, low = split_three(value)
    ref[index, 0:16, :] = jnp.concatenate([high, middle], axis=0).astype(BF16)
    ref[index, 16:32, :] = jnp.concatenate([low, jnp.zeros_like(low)], axis=0).astype(BF16)


def matrix_parts(value, axis):
    high = value.astype(BF16)
    return jnp.concatenate([high, (value - high.astype(F32)).astype(BF16)], axis=axis)


def matrix_product(left, right):
    full = jnp.dot(left, right, preferred_element_type=F32)
    cross = full[0:BS, BS : 2 * BS] + full[BS : 2 * BS, 0:BS] + full[BS : 2 * BS, BS : 2 * BS]
    return full[0:BS, 0:BS] + cross


def product(parts, matrix):
    full = lax.dot_general(
        parts, matrix, (((1,), (0,)), ((), ())), preferred_element_type=F32
    )
    high, middle, low = full[0:8], full[8:16], full[16:24]
    smallest = low[:, 0:BS] + middle[:, BS : 2 * BS]
    return high[:, 0:BS] + (middle[:, 0:BS] + high[:, BS : 2 * BS] + smallest)


def kernel(
    shape,
    blocks_ref,
    rows_hbm,
    cols_hbm,
    right_ref,
    near_ref,
    inverse_ref,
    both_ref,
    rows_ref,
    cols_ref,
    right_in,
    near_in,
    inverse_in,
    near_w,
    mixed_w,
    inverse_parts,
    ext_parts,
    field,
    picked,
    landed,
    dots,
    landed_dots,
    state,
    scalars,
    early,
    load_sem,
    swap_send,
    swap_recv,
    sum_send,
    sum_recv,
):
    size_x, size_z, size_y = shape
    patches = size_x * size_z * size_y
    patch = lax.axis_index("patch")
    core = lax.axis_index("grp")
    place_y = lax.rem(patch, size_y)
    place_z = lax.rem(lax.div(patch, size_y), size_z)
    place_x = lax.div(patch, size_y * size_z)
    before = lax.rem(patch + (patches - 1), patches)
    after = lax.rem(patch + 1, patches)
    other = 1 - core

    counts = (2 * size_z, size_x * size_y)

    def member(phase, offset):
        if phase == 0:
            place = lax.rem(place_z * 2 + core + offset, counts[0])
            spot_z, spot_core = lax.div(place, 2), lax.rem(place, 2)
            return ((place_x * size_z + spot_z) * size_y + place_y, spot_core)
        place = lax.rem(place_x * size_y + place_y + offset, counts[1])
        spot_x, spot_y = lax.div(place, size_y), lax.rem(place, size_y)
        return ((spot_x * size_z + place_z) * size_y + spot_y, core)

    barrier = pltpu.get_barrier_semaphore()
    greeted = 0
    for target in ((patch, other), (before, core), (before, other), (after, core), (after, other)):
        pl.semaphore_signal(barrier, inc=1, device_id=target, device_id_type=MESH)
        greeted += 1
    loads = [pltpu.make_async_copy(right_ref, right_in, load_sem.at[0])]
    loads += [pltpu.make_async_copy(inverse_ref.at[0], inverse_in, load_sem.at[1])]
    loads += [
        pltpu.make_async_copy(near_ref.at[b], near_in.at[b], load_sem.at[2 + b])
        for b in range(NB)
    ]
    loads += [
        pltpu.make_async_copy(source, target, load_sem.at[2 + NB + i])
        for i, (source, target) in enumerate(((rows_hbm, rows_ref), (cols_hbm, cols_ref)))
    ]
    for load in loads[2 + NB :] + loads[: 2 + NB]:
        load.start()

    for phase in range(2):
        for offset in range(1, counts[phase]):
            pl.semaphore_signal(
                barrier, inc=1, device_id=member(phase, offset), device_id_type=MESH
            )
            greeted += 1

    for load in loads[2 + NB :]:
        load.wait()
    first_slot = core * NB
    live = [
        jnp.where(first_slot + s < blocks_ref[0], jnp.float32(1), jnp.float32(0))
        for s in range(NB)
    ]
    lane = lax.broadcasted_iota(jnp.int32, (ROWS, BS), 1)
    case = lax.broadcasted_iota(jnp.int32, (ROWS, BS), 0)

    def sent_rows(way):
        found = []
        for o in range(NB):
            row = rows_ref[0, way, o]
            inside = jnp.logical_and(row >= first_slot, row < first_slot + NB)
            found.append(
                (jnp.bitwise_and(row, NB - 1), jnp.where(inside, jnp.float32(1), jnp.float32(0)))
            )
        return found

    sent = (sent_rows(0), sent_rows(1))
    far = jnp.where(place_y == 0, 1, 0)
    near = 1 - far

    def swap_copies(kind):
        plan = [(field.at[kind], 4, (patch, other))]
        for way in (near, far):
            neighbour = jnp.where(way == 1, before, after)
            plan = [
                (picked.at[kind, way], 2 * way, (neighbour, core)),
                (picked.at[kind, way], 2 * way + 1, (neighbour, other)),
            ] + plan
        return [
            pltpu.make_async_remote_copy(
                src_ref=source,
                dst_ref=landed.at[kind, slot],
                send_sem=swap_send.at[kind, slot],
                recv_sem=swap_recv.at[kind, slot],
                device_id=target,
                device_id_type=MESH,
            )
            for source, slot, target in plan
        ]

    def start_swap(kind):
        copies = swap_copies(kind)
        for way in range(2):
            for o in range(NB):
                row, mine = sent[way][o]
                picked[kind, way, o] = field[kind, row] * mine
        for copy in copies:
            copy.start()

    def sum_copies(parity, phase):
        return [
            pltpu.make_async_remote_copy(
                src_ref=dots.at[parity, phase],
                dst_ref=landed_dots.at[parity, phase, offset],
                send_sem=sum_send.at[parity, phase, offset],
                recv_sem=sum_recv.at[parity, phase, offset],
                device_id=member(phase, offset),
                device_id_type=MESH,
            )
            for offset in range(1, counts[phase])
        ]

    def finish_sum(parity, phase):
        total = dots[parity, phase]
        for offset, copy in enumerate(sum_copies(parity, phase), 1):
            copy.wait_recv()
            total = total + landed_dots[parity, phase, offset]
        return total

    def end_sends(copies):
        for copy in copies:
            copy.wait_send()

    def landing(kind, slot):
        return pltpu.make_async_remote_copy(
            src_ref=landed.at[kind, slot],
            dst_ref=landed.at[kind, slot],
            send_sem=swap_send.at[kind, slot],
            recv_sem=swap_recv.at[kind, slot],
            device_id=(patch, other),
            device_id_type=MESH,
        )

    def extend_inside(kind):
        for s in range(NB):
            store_parts(ext_parts, first_slot + s, field[kind, s])
        landing(kind, 4).wait_recv()
        for s in range(NB):
            store_parts(ext_parts, other * NB + s, landed[kind, 4, s])

    def extend_outside(kind):
        for way in (far, near):
            landing(kind, 2 * way).wait_recv()
            landing(kind, 2 * way + 1).wait_recv()
            for o in range(NB):
                value = landed[kind, 2 * way, o] + landed[kind, 2 * way + 1, o]
                store_parts(ext_parts, PB + NB * way + o, value)

    def apply_blocks(weights, b):
        gathered = jnp.concatenate([ext_parts[cols_ref[b, k]] for k in range(NEAR)], axis=1)
        return product(gathered, weights[b]) * live[b]

    def dot_lanes(pairs, first=0):
        tile = jnp.zeros((ROWS, BS), F32)
        for q, (left, right) in enumerate(pairs, first):
            partial = left[0] * right[0]
            for s in range(1, NB):
                partial = partial + left[s] * right[s]
            total = jnp.sum(partial, axis=1, keepdims=True)
            tile = jnp.where(lane == q * ROWS + case, total, tile)
        return tile

    def in_row(tile):
        return jnp.sum(tile, axis=0, keepdims=True)

    def pick(tile, q):
        mine = jnp.where(lane == q * ROWS + case, jnp.broadcast_to(tile, (ROWS, BS)), 0.0)
        return jnp.broadcast_to(jnp.sum(mine, axis=1, keepdims=True), (ROWS, BS))

    loads[0].wait()
    empty = jnp.zeros((ROWS - NRHS, BS), F32)
    for s in range(NB):
        value = jnp.concatenate([right_in[:, s, :], empty], axis=0) * live[s]
        field[0, s] = value
        state[0, s] = value
    pl.semaphore_wait(barrier, greeted)
    start_swap(0)
    loads[1].wait()
    for e in range(NE):
        inverse_parts[e] = matrix_parts(inverse_in[e], 1)

    @pl.loop(0, NB)
    def _(b):
        pltpu.make_async_copy(near_ref.at[b], near_in.at[b], load_sem.at[2 + b]).wait()
        own = inverse_in[first_slot + b]
        own_parts = matrix_parts(own, 0)
        for k in range(NEAR):
            rows = slice(k * BS, (k + 1) * BS)
            block = near_in[b, k]
            left = matrix_product(own_parts, matrix_parts(block, 1))
            value = -matrix_product(matrix_parts(left, 0), inverse_parts[cols_ref[b, k]])
            if k == 0:
                value = 2.0 * own + value
            mixed_w[b, rows, :] = matrix_parts(value.T, 1)

    R, RAW1, Z1, FIRST, ZETA1, MAPPED1, SECOND, ZETA2, MAPPED2, RAWZ, RAWM, SOL, PART = range(13)
    NORM, INVERSE, SQUARE, LEAD, LEAD_NORM, FACTOR = range(6)

    def get(index):
        return [state[index, s] for s in range(NB)]

    def put(index, values):
        for s in range(NB):
            state[index, s] = values[s]

    def of_field(kind):
        return [field[kind, s] for s in range(NB)]

    def combine(*terms):
        out = []
        for s in range(NB):
            value = None
            for coefficient, vector in terms:
                term = vector[s] if coefficient is None else coefficient * vector[s]
                value = term if value is None else value + term
            out.append(value)
        return out

    def lead(total):
        square, mixed, mapped_square = [pick(total, q) for q in range(3)]
        norm = jnp.sqrt(square + EPSILON)
        inverse = 1.0 / norm
        first_square = square * inverse * inverse
        lead_dot = mixed * inverse * inverse
        reduced = mapped_square * inverse * inverse - lead_dot * lead_dot * (2.0 - first_square)
        lead_norm = jnp.sqrt(jnp.maximum(reduced, 0.0) + EPSILON)
        scale = 1.0 / lead_norm
        for index, value in (
            (NORM, norm),
            (INVERSE, inverse),
            (SQUARE, first_square),
            (LEAD, lead_dot),
            (LEAD_NORM, lead_norm),
        ):
            scalars[index] = value
        first = combine((inverse, get(R)))
        mapped_one = combine((inverse, get(RAW1)))
        zeta_one = combine((inverse, get(Z1)))
        raw_zeta = combine((inverse, of_field(1)))
        second = combine((scale, combine((None, mapped_one), (-lead_dot, first))))
        put(FIRST, first)
        put(MAPPED1, mapped_one)
        put(ZETA1, zeta_one)
        put(RAWZ, raw_zeta)
        put(SECOND, second)
        put(ZETA2, combine((scale, combine((None, raw_zeta), (-lead_dot, zeta_one)))))
        scalars[FACTOR] = -scale * inverse
        put(PART, combine((-scale * lead_dot, mapped_one)))
        early[...] = dot_lanes([(first, second), (second, second)], 3)

    def coefficients(total):
        upper, lower, square, cross, second_square = [pick(total, q) for q in range(5)]
        tail = (
            square
            - upper * upper * (2.0 - scalars[SQUARE])
            - lower * lower * (2.0 - second_square)
            + 2.0 * upper * lower * cross
        )
        tail_norm = jnp.sqrt(jnp.maximum(tail, 0.0) + EPSILON)
        return least_squares(
            scalars[NORM], scalars[LEAD], scalars[LEAD_NORM], upper, lower, tail_norm
        )

    def restart(total):
        one, two = coefficients(total)
        norm = scalars[NORM]
        mapped_one, zeta_one = get(MAPPED1), get(ZETA1)
        put(SOL, combine((one, zeta_one), (two, get(ZETA2))))
        put(R, combine((None, get(R)), (-one, mapped_one), (-two, get(MAPPED2))))
        put(Z1, combine((norm, zeta_one), (-one, get(RAWZ)), (-two, of_field(1))))
        put(PART, combine((norm, mapped_one), (-one, get(RAWM))))
        scalars[FACTOR] = two

    @pl.loop(0, 2 * CYCLES)
    def _(i):
        parity = lax.rem(i, 2)
        extend_inside(0)

        @pl.when(i >= 1)
        def _():
            dots[parity, 1] = finish_sum(parity, 0)
            copies = sum_copies(parity, 1)
            for copy in copies:
                copy.start()
            end_sends(sum_copies(parity, 0))

        extend_outside(0)
        for b in range(NB):
            field[1, b] = apply_blocks(mixed_w, b)
        start_swap(1)
        end_sends(swap_copies(0))

        @pl.when(i == 0)
        def _():
            for b in range(NB):
                for k in range(NEAR):
                    near_w[b, k * BS : (k + 1) * BS, :] = matrix_parts(near_in[b, k].T, 1)
            put(Z1, of_field(1))

        extend_inside(1)

        @pl.when(parity == 1)
        def _():
            lead(finish_sum(1, 1))
            end_sends(sum_copies(1, 1))

        @pl.when(i == 2)
        def _():
            restart(finish_sum(0, 1))
            end_sends(sum_copies(0, 1))

        extend_outside(1)
        for b in range(NB):
            field[0, b] = apply_blocks(near_w, b)

        @pl.when(i >= 1)
        def _():
            mapped = of_field(0)
            put(RAWM, combine((scalars[INVERSE], mapped)))
            mapped = combine((None, get(PART)), (-scalars[FACTOR], mapped))
            for s in range(NB):
                field[0, s] = mapped[s]

        @pl.when(i < 2 * CYCLES - 1)
        def _():
            start_swap(0)

        @pl.when(parity == 0)
        def _():
            mapped, current = of_field(0), get(R)
            dots[1, 0] = in_row(
                dot_lanes([(current, current), (current, mapped), (mapped, mapped)])
            )
            for copy in sum_copies(1, 0):
                copy.start()
            put(RAW1, mapped)

        @pl.when(parity == 1)
        def _():
            mapped = of_field(0)
            dots[0, 0] = in_row(
                dot_lanes([(mapped, get(FIRST)), (mapped, get(SECOND)), (mapped, mapped)])
                + early[...]
            )
            for copy in sum_copies(0, 0):
                copy.start()
            put(MAPPED2, mapped)

        end_sends(swap_copies(1))

    dots[0, 1] = finish_sum(0, 0)
    for copy in sum_copies(0, 1):
        copy.start()
    end_sends(sum_copies(0, 0))
    one, two = coefficients(finish_sum(0, 1))
    answer = combine((None, get(SOL)), (one, get(ZETA1)), (two, get(ZETA2)))
    left = combine((None, get(R)), (-one, get(MAPPED1)), (-two, get(MAPPED2)))
    for s in range(NB):
        both_ref[0, :, s, :] = answer[s][0:NRHS]
        both_ref[1, :, s, :] = left[s][0:NRHS]
    end_sends(sum_copies(0, 1))


def factors(patches):
    known = {128: (4, 8, 4), 8: (2, 2, 2), 4: (1, 2, 2)}
    return known.get(patches, (1, patches, 1))


def local(shape, right_side, patch_blocks, send_rows, near_cols, near_blocks, inverses):
    counts = (2 * shape[1], shape[0] * shape[2])
    most = max(counts)
    field = jax.ShapeDtypeStruct((2,) + right_side.shape, F32)
    vmem = pl.BlockSpec(memory_space=pltpu.VMEM)
    hbm = pl.BlockSpec(memory_space=pltpu.HBM)
    send_rows, near_cols, right_side, near_blocks, inverses = [
        pltpu.with_memory_space_constraint(value, pltpu.HBM)
        for value in (send_rows, near_cols, right_side, near_blocks, inverses)
    ]
    both = pl.pallas_call(
        functools.partial(kernel, shape),
        out_shape=field,
        in_specs=[pl.BlockSpec(memory_space=pltpu.SMEM)] + [hbm] * 5,
        out_specs=vmem,
        scratch_shapes=[
            pltpu.SMEM((1, 2, NB), jnp.int32),
            pltpu.SMEM((NB, NEAR), jnp.int32),
            pltpu.VMEM((NRHS, NB, BS), F32),
            pltpu.VMEM((NB, NEAR, BS, BS), F32),
            pltpu.VMEM((NE, BS, BS), F32),
            pltpu.VMEM((NB, NEAR * BS, 2 * BS), BF16),
            pltpu.VMEM((NB, NEAR * BS, 2 * BS), BF16),
            pltpu.VMEM((NE, BS, 2 * BS), BF16),
            pltpu.VMEM((NE, 32, BS), BF16),
            pltpu.VMEM((2, NB, ROWS, BS), F32),
            pltpu.VMEM((2, 2, NB, ROWS, BS), F32),
            pltpu.VMEM((2, 5, NB, ROWS, BS), F32),
            pltpu.VMEM((2, 2, 1, BS), F32),
            pltpu.VMEM((2, 2, most, 1, BS), F32),
            pltpu.VMEM((13, NB, ROWS, BS), F32),
            pltpu.VMEM((6, ROWS, BS), F32),
            pltpu.VMEM((ROWS, BS), F32),
            pltpu.SemaphoreType.DMA((4 + NB,)),
            pltpu.SemaphoreType.DMA((2, 5)),
            pltpu.SemaphoreType.DMA((2, 5)),
            pltpu.SemaphoreType.DMA((2, 2, most)),
            pltpu.SemaphoreType.DMA((2, 2, most)),
        ],
        compiler_params=pltpu.CompilerParams(
            collective_id=0, has_side_effects=True, vmem_limit_bytes=32 * 1024 * 1024
        ),
        name="gmres",
    )(patch_blocks, send_rows, near_cols, right_side, near_blocks, inverses)
    return both[0], both[1]


def solution(mesh):
    in_specs = (
        P(None, ("patch", "grp"), None),
        P("patch"),
        P("patch", None, None),
        P(("patch", "grp"), None),
        P(("patch", "grp"), None, None, None),
        P("patch", None, None, None),
    )
    out_specs = (P(None, ("patch", "grp"), None), P(None, ("patch", "grp"), None))
    shape = factors(mesh.shape["patch"])
    return jax.shard_map(
        functools.partial(local, shape),
        mesh=mesh,
        in_specs=in_specs,
        out_specs=out_specs,
        check_vma=False,
    )
```

```python
import functools

import jax
import jax.numpy as jnp
from jax import lax
from jax.experimental import pallas as pl
from jax.experimental.pallas import tpu as pltpu
from jax.sharding import PartitionSpec as P

CYCLES = 2
EPSILON = 1e-06
NB = 4
PB = 8
NE = 16
NEAR = 10
BS = 128
NRHS = 6
ROWS = 8
MESH = pl.DeviceIdType.MESH
F32 = jnp.float32
BF16 = jnp.bfloat16


def least_squares(start_norm, lead_dot, lead_norm, upper_dot, lower_dot, tail_norm):
    radius_one = jnp.sqrt(lead_dot * lead_dot + lead_norm * lead_norm)
    cosine_one = lead_dot / radius_one
    sine_one = lead_norm / radius_one
    carried = cosine_one * upper_dot + sine_one * lower_dot
    rotated = cosine_one * lower_dot - sine_one * upper_dot
    radius_two = jnp.sqrt(rotated * rotated + tail_norm * tail_norm)
    coef_two = -start_norm * sine_one * rotated / (radius_two * radius_two)
    coef_one = (start_norm * cosine_one - carried * coef_two) / radius_one
    return (coef_one, coef_two)


def split_three(value):
    high = value.astype(BF16).astype(F32)
    rest = value - high
    middle = rest.astype(BF16).astype(F32)
    return high, middle, rest - middle


def vector_parts(value):
    high, middle, low = split_three(value)
    first = jnp.concatenate([high, middle], axis=0).astype(BF16)
    second = jnp.concatenate([low, jnp.zeros_like(low)], axis=0).astype(BF16)
    return jnp.concatenate([first, second], axis=0)


def matrix_parts(value, axis, count=2):
    parts = []
    for _ in range(count):
        parts.append(value.astype(BF16))
        value = value - parts[-1].astype(F32)
    return jnp.concatenate(parts, axis=axis)


def matrix_product(left, right):
    full = jnp.dot(left, right, preferred_element_type=F32)
    cross = full[0:BS, BS : 2 * BS] + full[BS : 2 * BS, 0:BS] + full[BS : 2 * BS, BS : 2 * BS]
    return full[0:BS, 0:BS] + cross


def gather_parts(full):
    high, middle, low = full[0:8], full[8:16], full[16:24]
    smallest = low[:, 0:BS] + middle[:, BS : 2 * BS]
    if full.shape[1] == 3 * BS:
        smallest = smallest + high[:, 2 * BS : 3 * BS]
    return high[:, 0:BS] + (middle[:, 0:BS] + high[:, BS : 2 * BS] + smallest)


def kernel(
    shape,
    blocks_ref,
    rows_hbm,
    cols_hbm,
    right_ref,
    near_ref,
    inverse_ref,
    both_ref,
    rows_ref,
    cols_ref,
    right_in,
    near_in,
    inverse_in,
    mixed_in,
    mixed_w,
    near_dense,
    mixed_dense,
    inverse_parts,
    ext_parts,
    field,
    picked,
    landed,
    dots,
    landed_dots,
    state,
    scalars,
    early,
    load_sem,
    swap_send,
    swap_recv,
    sum_send,
    sum_recv,
):
    size_x, size_z, size_y = shape
    patches = size_x * size_z * size_y
    patch = lax.axis_index("patch")
    core = lax.axis_index("grp")
    place_y = lax.rem(patch, size_y)
    place_z = lax.rem(lax.div(patch, size_y), size_z)
    place_x = lax.div(patch, size_y * size_z)
    before = lax.rem(patch + (patches - 1), patches)
    after = lax.rem(patch + 1, patches)
    other = 1 - core

    counts = (2 * size_z, size_x * size_y)

    def member(phase, offset):
        if phase == 0:
            place = lax.rem(place_z * 2 + core + offset, counts[0])
            spot_z, spot_core = lax.div(place, 2), lax.rem(place, 2)
            return ((place_x * size_z + spot_z) * size_y + place_y, spot_core)
        place = lax.rem(place_x * size_y + place_y + offset, counts[1])
        spot_x, spot_y = lax.div(place, size_y), lax.rem(place, size_y)
        return ((spot_x * size_z + place_z) * size_y + spot_y, core)

    barrier = pltpu.get_barrier_semaphore()
    greeted = 0
    for target in ((patch, other), (before, core), (before, other), (after, core), (after, other)):
        pl.semaphore_signal(barrier, inc=1, device_id=target, device_id_type=MESH)
        greeted += 1
    loads = [pltpu.make_async_copy(right_ref, right_in, load_sem.at[0])]
    loads += [pltpu.make_async_copy(inverse_ref.at[0], inverse_in, load_sem.at[1])]
    loads += [
        pltpu.make_async_copy(near_ref.at[b], near_in.at[b], load_sem.at[2 + b])
        for b in range(NB)
    ]
    loads += [
        pltpu.make_async_copy(source, target, load_sem.at[2 + NB + i])
        for i, (source, target) in enumerate(((rows_hbm, rows_ref), (cols_hbm, cols_ref)))
    ]
    for load in loads[2 + NB :] + loads[: 2 + NB]:
        load.start()

    for phase in range(2):
        for offset in range(1, counts[phase]):
            pl.semaphore_signal(
                barrier, inc=1, device_id=member(phase, offset), device_id_type=MESH
            )
            greeted += 1

    for load in loads[2 + NB :]:
        load.wait()
    first_slot = core * NB
    live = [
        jnp.where(first_slot + s < blocks_ref[0], jnp.float32(1), jnp.float32(0))
        for s in range(NB)
    ]
    lane = lax.broadcasted_iota(jnp.int32, (ROWS, BS), 1)
    case = lax.broadcasted_iota(jnp.int32, (ROWS, BS), 0)

    def sent_rows(way):
        found = []
        for o in range(NB):
            row = rows_ref[0, way, o]
            inside = jnp.logical_and(row >= first_slot, row < first_slot + NB)
            found.append(
                (jnp.bitwise_and(row, NB - 1), jnp.where(inside, jnp.float32(1), jnp.float32(0)))
            )
        return found

    sent = (sent_rows(0), sent_rows(1))
    far = jnp.where(place_y == 0, 1, 0)
    near = 1 - far

    def swap_copies(kind):
        plan = [(field.at[kind], 4, (patch, other))]
        for way in (near, far):
            neighbour = jnp.where(way == 1, before, after)
            plan = [
                (picked.at[kind, way], 2 * way, (neighbour, core)),
                (picked.at[kind, way], 2 * way + 1, (neighbour, other)),
            ] + plan
        return [
            pltpu.make_async_remote_copy(
                src_ref=source,
                dst_ref=landed.at[kind, slot],
                send_sem=swap_send.at[kind, slot],
                recv_sem=swap_recv.at[kind, slot],
                device_id=target,
                device_id_type=MESH,
            )
            for source, slot, target in plan
        ]

    def start_swap(kind):
        copies = swap_copies(kind)
        for way in range(2):
            for o in range(NB):
                row, mine = sent[way][o]
                picked[kind, way, o] = field[kind, row] * mine
        for copy in copies:
            copy.start()

    def sum_copies(parity, phase):
        return [
            pltpu.make_async_remote_copy(
                src_ref=dots.at[parity, phase],
                dst_ref=landed_dots.at[parity, phase, offset],
                send_sem=sum_send.at[parity, phase, offset],
                recv_sem=sum_recv.at[parity, phase, offset],
                device_id=member(phase, offset),
                device_id_type=MESH,
            )
            for offset in range(1, counts[phase])
        ]

    def finish_sum(parity, phase):
        total = dots[parity, phase]
        for offset, copy in enumerate(sum_copies(parity, phase), 1):
            copy.wait_recv()
            total = total + landed_dots[parity, phase, offset]
        return total

    def end_sends(copies):
        for copy in copies:
            copy.wait_send()

    def landing(kind, slot):
        return pltpu.make_async_remote_copy(
            src_ref=landed.at[kind, slot],
            dst_ref=landed.at[kind, slot],
            send_sem=swap_send.at[kind, slot],
            recv_sem=swap_recv.at[kind, slot],
            device_id=(patch, other),
            device_id_type=MESH,
        )

    def own_blocks(kind):
        return [field[kind, s] for s in range(NB)]

    def core_blocks(kind):
        landing(kind, 4).wait_recv()
        return [landed[kind, 4, s] for s in range(NB)]

    def margin_blocks(kind, way):
        landing(kind, 2 * way).wait_recv()
        landing(kind, 2 * way + 1).wait_recv()
        return [landed[kind, 2 * way, o] + landed[kind, 2 * way + 1, o] for o in range(NB)]

    def apply_first():
        for base, values in (
            (first_slot, own_blocks(0)),
            (other * NB, core_blocks(0)),
            (PB + NB * far, margin_blocks(0, far)),
            (PB + NB * near, margin_blocks(0, near)),
        ):
            for o in range(NB):
                ext_parts[base + o] = vector_parts(values[o])
        for b in range(NB):
            gathered = jnp.concatenate([ext_parts[cols_ref[b, k]] for k in range(NEAR)], axis=1)
            full = jnp.dot(gathered, mixed_w[b], preferred_element_type=F32)
            field[1, b] = gather_parts(full) * live[b]

    def apply_group(weights, base, values):
        parts = jnp.concatenate([vector_parts(value) for value in values], axis=1)
        rows = pl.ds(pl.multiple_of(base * BS, NB * BS), NB * BS)
        full = jnp.dot(parts, weights[rows, :], preferred_element_type=F32)
        width = full.shape[1] // NB
        return [gather_parts(full[:, width * b : width * (b + 1)]) for b in range(NB)]

    def apply_dense(kind, weights, meanwhile):
        total = apply_group(weights, first_slot, own_blocks(kind))
        part = apply_group(weights, other * NB, core_blocks(kind))
        total = [total[b] + part[b] for b in range(NB)]
        part = apply_group(weights, PB + NB * far, margin_blocks(kind, far))
        total = [total[b] + part[b] for b in range(NB)]
        meanwhile()
        part = apply_group(weights, PB + NB * near, margin_blocks(kind, near))
        for b in range(NB):
            field[1 - kind, b] = total[b] + part[b]

    def make_dense(weights, blocks, turned):
        @pl.loop(0, NE)
        def _(e):
            rows = pl.ds(pl.multiple_of(e * BS, BS), BS)
            for b in range(NB):
                total = jnp.zeros((BS, BS), F32)
                for k in range(NEAR):
                    total = total + blocks[b, k] * jnp.where(cols_ref[b, k] == e, live[b], 0.0)
                if not turned:
                    total = total.T
                width = weights.shape[1] // NB
                columns = slice(width * b, width * (b + 1))
                weights[rows, columns] = matrix_parts(total, 1, width // BS)

    def dot_lanes(pairs, first=0):
        tile = jnp.zeros((ROWS, BS), F32)
        for q, (left, right) in enumerate(pairs, first):
            partial = left[0] * right[0]
            for s in range(1, NB):
                partial = partial + left[s] * right[s]
            total = jnp.sum(partial, axis=1, keepdims=True)
            tile = jnp.where(lane == q * ROWS + case, total, tile)
        return tile

    def in_row(tile):
        return jnp.sum(tile, axis=0, keepdims=True)

    def pick(tile, q):
        mine = jnp.where(lane == q * ROWS + case, jnp.broadcast_to(tile, (ROWS, BS)), 0.0)
        return jnp.broadcast_to(jnp.sum(mine, axis=1, keepdims=True), (ROWS, BS))

    loads[0].wait()
    empty = jnp.zeros((ROWS - NRHS, BS), F32)
    for s in range(NB):
        value = jnp.concatenate([right_in[:, s, :], empty], axis=0) * live[s]
        field[0, s] = value
        state[0, s] = value
    pl.semaphore_wait(barrier, greeted)
    start_swap(0)
    loads[1].wait()
    for e in range(NE):
        inverse_parts[e] = matrix_parts(inverse_in[e], 1)

    @pl.loop(0, NB)
    def _(b):
        pltpu.make_async_copy(near_ref.at[b], near_in.at[b], load_sem.at[2 + b]).wait()
        own = inverse_in[first_slot + b]
        own_parts = matrix_parts(own, 0)
        for k in range(NEAR):
            rows = slice(k * BS, (k + 1) * BS)
            block = near_in[b, k]
            left = matrix_product(own_parts, matrix_parts(block, 1))
            value = -matrix_product(matrix_parts(left, 0), inverse_parts[cols_ref[b, k]])
            if k == 0:
                value = 2.0 * own + value
            value = value.T
            mixed_in[b, k] = value
            mixed_w[b, rows, :] = matrix_parts(value, 1, 3)

    R, RAW1, Z1, FIRST, ZETA1, MAPPED1, SECOND, ZETA2, MAPPED2, RAWZ, RAWM, SOL, PART = range(13)
    NORM, INVERSE, SQUARE, LEAD, LEAD_NORM, FACTOR = range(6)

    def get(index):
        return [state[index, s] for s in range(NB)]

    def put(index, values):
        for s in range(NB):
            state[index, s] = values[s]

    def of_field(kind):
        return [field[kind, s] for s in range(NB)]

    def combine(*terms):
        out = []
        for s in range(NB):
            value = None
            for coefficient, vector in terms:
                term = vector[s] if coefficient is None else coefficient * vector[s]
                value = term if value is None else value + term
            out.append(value)
        return out

    def lead(total):
        square, mixed, mapped_square = [pick(total, q) for q in range(3)]
        norm = jnp.sqrt(square + EPSILON)
        inverse = 1.0 / norm
        first_square = square * inverse * inverse
        lead_dot = mixed * inverse * inverse
        reduced = mapped_square * inverse * inverse - lead_dot * lead_dot * (2.0 - first_square)
        lead_norm = jnp.sqrt(jnp.maximum(reduced, 0.0) + EPSILON)
        scale = 1.0 / lead_norm
        for index, value in (
            (NORM, norm),
            (INVERSE, inverse),
            (SQUARE, first_square),
            (LEAD, lead_dot),
            (LEAD_NORM, lead_norm),
        ):
            scalars[index] = value
        first = combine((inverse, get(R)))
        mapped_one = combine((inverse, get(RAW1)))
        zeta_one = combine((inverse, get(Z1)))
        raw_zeta = combine((inverse, of_field(1)))
        second = combine((scale, combine((None, mapped_one), (-lead_dot, first))))
        put(FIRST, first)
        put(MAPPED1, mapped_one)
        put(ZETA1, zeta_one)
        put(RAWZ, raw_zeta)
        put(SECOND, second)
        put(ZETA2, combine((scale, combine((None, raw_zeta), (-lead_dot, zeta_one)))))
        scalars[FACTOR] = -scale * inverse
        put(PART, combine((-scale * lead_dot, mapped_one)))
        early[...] = dot_lanes([(first, second), (second, second)], 3)

    def coefficients(total):
        upper, lower, square, cross, second_square = [pick(total, q) for q in range(5)]
        tail = (
            square
            - upper * upper * (2.0 - scalars[SQUARE])
            - lower * lower * (2.0 - second_square)
            + 2.0 * upper * lower * cross
        )
        tail_norm = jnp.sqrt(jnp.maximum(tail, 0.0) + EPSILON)
        return least_squares(
            scalars[NORM], scalars[LEAD], scalars[LEAD_NORM], upper, lower, tail_norm
        )

    def restart(total):
        one, two = coefficients(total)
        norm = scalars[NORM]
        mapped_one, zeta_one = get(MAPPED1), get(ZETA1)
        put(SOL, combine((one, zeta_one), (two, get(ZETA2))))
        put(R, combine((None, get(R)), (-one, mapped_one), (-two, get(MAPPED2))))
        put(Z1, combine((norm, zeta_one), (-one, get(RAWZ)), (-two, of_field(1))))
        put(PART, combine((norm, mapped_one), (-one, get(RAWM))))
        scalars[FACTOR] = two

    @pl.loop(0, 2 * CYCLES)
    def _(i):
        parity = lax.rem(i, 2)

        def pass_sum():
            dots[parity, 1] = finish_sum(parity, 0)
            for copy in sum_copies(parity, 1):
                copy.start()
            end_sends(sum_copies(parity, 0))

        def use_sum():
            @pl.when(parity == 1)
            def _():
                lead(finish_sum(1, 1))
                end_sends(sum_copies(1, 1))

            @pl.when(i == 2)
            def _():
                restart(finish_sum(0, 1))
                end_sends(sum_copies(0, 1))

        @pl.when(i == 0)
        def _():
            apply_first()

        @pl.when(i >= 1)
        def _():
            apply_dense(0, mixed_dense, pass_sum)

        start_swap(1)
        end_sends(swap_copies(0))

        @pl.when(i == 0)
        def _():
            make_dense(near_dense, near_in, False)
            put(Z1, of_field(1))

        apply_dense(1, near_dense, use_sum)

        @pl.when(i >= 1)
        def _():
            mapped = of_field(0)
            put(RAWM, combine((scalars[INVERSE], mapped)))
            mapped = combine((None, get(PART)), (-scalars[FACTOR], mapped))
            for s in range(NB):
                field[0, s] = mapped[s]

        @pl.when(i < 2 * CYCLES - 1)
        def _():
            start_swap(0)

        @pl.when(parity == 0)
        def _():
            mapped, current = of_field(0), get(R)
            dots[1, 0] = in_row(
                dot_lanes([(current, current), (current, mapped), (mapped, mapped)])
            )
            for copy in sum_copies(1, 0):
                copy.start()
            put(RAW1, mapped)

        @pl.when(parity == 1)
        def _():
            mapped = of_field(0)
            dots[0, 0] = in_row(
                dot_lanes([(mapped, get(FIRST)), (mapped, get(SECOND)), (mapped, mapped)])
                + early[...]
            )
            for copy in sum_copies(0, 0):
                copy.start()
            put(MAPPED2, mapped)

        end_sends(swap_copies(1))

        @pl.when(i == 0)
        def _():
            make_dense(mixed_dense, mixed_in, True)

    dots[0, 1] = finish_sum(0, 0)
    for copy in sum_copies(0, 1):
        copy.start()
    end_sends(sum_copies(0, 0))
    one, two = coefficients(finish_sum(0, 1))
    answer = combine((None, get(SOL)), (one, get(ZETA1)), (two, get(ZETA2)))
    left = combine((None, get(R)), (-one, get(MAPPED1)), (-two, get(MAPPED2)))
    for s in range(NB):
        both_ref[0, :, s, :] = answer[s][0:NRHS]
        both_ref[1, :, s, :] = left[s][0:NRHS]
    end_sends(sum_copies(0, 1))


def factors(patches):
    known = {128: (4, 8, 4), 8: (2, 2, 2), 4: (1, 2, 2)}
    return known.get(patches, (1, patches, 1))


def local(shape, right_side, patch_blocks, send_rows, near_cols, near_blocks, inverses):
    counts = (2 * shape[1], shape[0] * shape[2])
    most = max(counts)
    field = jax.ShapeDtypeStruct((2,) + right_side.shape, F32)
    vmem = pl.BlockSpec(memory_space=pltpu.VMEM)
    hbm = pl.BlockSpec(memory_space=pltpu.HBM)
    send_rows, near_cols, right_side, near_blocks, inverses = [
        pltpu.with_memory_space_constraint(value, pltpu.HBM)
        for value in (send_rows, near_cols, right_side, near_blocks, inverses)
    ]
    both = pl.pallas_call(
        functools.partial(kernel, shape),
        out_shape=field,
        in_specs=[pl.BlockSpec(memory_space=pltpu.SMEM)] + [hbm] * 5,
        out_specs=vmem,
        scratch_shapes=[
            pltpu.SMEM((1, 2, NB), jnp.int32),
            pltpu.SMEM((NB, NEAR), jnp.int32),
            pltpu.VMEM((NRHS, NB, BS), F32),
            pltpu.VMEM((NB, NEAR, BS, BS), F32),
            pltpu.VMEM((NE, BS, BS), F32),
            pltpu.VMEM((NB, NEAR, BS, BS), F32),
            pltpu.VMEM((NB, NEAR * BS, 3 * BS), BF16),
            pltpu.VMEM((NE * BS, NB * 2 * BS), BF16),
            pltpu.VMEM((NE * BS, NB * 3 * BS), BF16),
            pltpu.VMEM((NE, BS, 2 * BS), BF16),
            pltpu.VMEM((NE, 32, BS), BF16),
            pltpu.VMEM((2, NB, ROWS, BS), F32),
            pltpu.VMEM((2, 2, NB, ROWS, BS), F32),
            pltpu.VMEM((2, 5, NB, ROWS, BS), F32),
            pltpu.VMEM((2, 2, 1, BS), F32),
            pltpu.VMEM((2, 2, most, 1, BS), F32),
            pltpu.VMEM((13, NB, ROWS, BS), F32),
            pltpu.VMEM((6, ROWS, BS), F32),
            pltpu.VMEM((ROWS, BS), F32),
            pltpu.SemaphoreType.DMA((4 + NB,)),
            pltpu.SemaphoreType.DMA((2, 5)),
            pltpu.SemaphoreType.DMA((2, 5)),
            pltpu.SemaphoreType.DMA((2, 2, most)),
            pltpu.SemaphoreType.DMA((2, 2, most)),
        ],
        compiler_params=pltpu.CompilerParams(
            collective_id=0, has_side_effects=True, vmem_limit_bytes=32 * 1024 * 1024
        ),
        name="gmres",
    )(patch_blocks, send_rows, near_cols, right_side, near_blocks, inverses)
    return both[0], both[1]


def solution(mesh):
    in_specs = (
        P(None, ("patch", "grp"), None),
        P("patch"),
        P("patch", None, None),
        P(("patch", "grp"), None),
        P(("patch", "grp"), None, None, None),
        P("patch", None, None, None),
    )
    out_specs = (P(None, ("patch", "grp"), None), P(None, ("patch", "grp"), None))
    shape = factors(mesh.shape["patch"])
    return jax.shard_map(
        functools.partial(local, shape),
        mesh=mesh,
        in_specs=in_specs,
        out_specs=out_specs,
        check_vma=False,
    )
```

```python
import functools

import jax
import jax.numpy as jnp
from jax import lax
from jax.experimental import pallas as pl
from jax.experimental.pallas import tpu as pltpu
from jax.sharding import PartitionSpec as P

CYCLES = 2
EPSILON = 1e-06
NB = 4
PB = 8
NE = 16
NEAR = 10
BS = 128
NRHS = 6
ROWS = 8
MESH = pl.DeviceIdType.MESH
F32 = jnp.float32
BF16 = jnp.bfloat16


def split_three(value):
    high = value.astype(BF16).astype(F32)
    rest = value - high
    middle = rest.astype(BF16).astype(F32)
    return high, middle, rest - middle


def vector_parts(value):
    high, middle, low = split_three(value)
    first = jnp.concatenate([high, middle], axis=0).astype(BF16)
    second = jnp.concatenate([low, jnp.zeros_like(low)], axis=0).astype(BF16)
    return jnp.concatenate([first, second], axis=0)


def matrix_parts(value, axis, count=2):
    parts = []
    for _ in range(count):
        parts.append(value.astype(BF16))
        value = value - parts[-1].astype(F32)
    return jnp.concatenate(parts, axis=axis)


def matrix_product(left, right):
    full = jnp.dot(left, right, preferred_element_type=F32)
    cross = full[0:BS, BS : 2 * BS] + full[BS : 2 * BS, 0:BS] + full[BS : 2 * BS, BS : 2 * BS]
    return full[0:BS, 0:BS] + cross


def gather_parts(full):
    high, middle, low = full[0:8], full[8:16], full[16:24]
    smallest = low[:, 0:BS] + middle[:, BS : 2 * BS]
    if full.shape[1] == 3 * BS:
        smallest = smallest + high[:, 2 * BS : 3 * BS]
    return high[:, 0:BS] + (middle[:, 0:BS] + high[:, BS : 2 * BS] + smallest)


def kernel(
    shape,
    blocks_ref,
    rows_hbm,
    cols_hbm,
    right_ref,
    near_ref,
    inverse_ref,
    both_ref,
    rows_ref,
    cols_ref,
    right_in,
    near_in,
    inverse_in,
    mixed_in,
    mixed_w,
    near_dense,
    mixed_dense,
    inverse_parts,
    ext_parts,
    field,
    picked,
    landed,
    dots,
    landed_dots,
    state,
    scalars,
    early,
    load_sem,
    swap_send,
    swap_recv,
    sum_send,
    sum_recv,
):
    size_x, size_z, size_y = shape
    patches = size_x * size_z * size_y
    patch = lax.axis_index("patch")
    core = lax.axis_index("grp")
    place_y = lax.rem(patch, size_y)
    place_z = lax.rem(lax.div(patch, size_y), size_z)
    place_x = lax.div(patch, size_y * size_z)
    before = lax.rem(patch + (patches - 1), patches)
    after = lax.rem(patch + 1, patches)
    other = 1 - core

    counts = (2 * size_z, size_x * size_y)

    def hops(offset, size):
        return min(offset, size - offset)

    offsets = (
        sorted(range(1, counts[0]), key=lambda o: -hops(o, counts[0])),
        sorted(
            range(1, counts[1]),
            key=lambda o: -hops(o // size_y, size_x) - hops(o % size_y, size_y),
        ),
    )

    def member(phase, offset):
        if phase == 0:
            place = lax.rem(place_z * 2 + core + offset, counts[0])
            spot_z, spot_core = lax.div(place, 2), lax.rem(place, 2)
            return ((place_x * size_z + spot_z) * size_y + place_y, spot_core)
        place = lax.rem(place_x * size_y + place_y + offset, counts[1])
        spot_x, spot_y = lax.div(place, size_y), lax.rem(place, size_y)
        return ((spot_x * size_z + place_z) * size_y + spot_y, core)

    barrier = pltpu.get_barrier_semaphore()
    greeted = 0
    for target in ((patch, other), (before, core), (before, other), (after, core), (after, other)):
        pl.semaphore_signal(barrier, inc=1, device_id=target, device_id_type=MESH)
        greeted += 1
    loads = [pltpu.make_async_copy(right_ref, right_in, load_sem.at[0])]
    loads += [pltpu.make_async_copy(inverse_ref.at[0], inverse_in, load_sem.at[1])]
    loads += [
        pltpu.make_async_copy(near_ref.at[b], near_in.at[b], load_sem.at[2 + b])
        for b in range(NB)
    ]
    loads += [
        pltpu.make_async_copy(source, target, load_sem.at[2 + NB + i])
        for i, (source, target) in enumerate(((rows_hbm, rows_ref), (cols_hbm, cols_ref)))
    ]
    for load in loads[2 + NB :] + loads[: 2 + NB]:
        load.start()

    for phase in range(2):
        for offset in offsets[phase]:
            pl.semaphore_signal(
                barrier, inc=1, device_id=member(phase, offset), device_id_type=MESH
            )
            greeted += 1

    for load in loads[2 + NB :]:
        load.wait()
    first_slot = core * NB
    live = [
        jnp.where(first_slot + s < blocks_ref[0], jnp.float32(1), jnp.float32(0))
        for s in range(NB)
    ]
    lane = lax.broadcasted_iota(jnp.int32, (ROWS, BS), 1)
    case = lax.broadcasted_iota(jnp.int32, (ROWS, BS), 0)

    def sent_rows(way):
        found = []
        for o in range(NB):
            row = rows_ref[0, way, o]
            inside = jnp.logical_and(row >= first_slot, row < first_slot + NB)
            found.append(
                (jnp.bitwise_and(row, NB - 1), jnp.where(inside, jnp.float32(1), jnp.float32(0)))
            )
        return found

    far = jnp.where(place_y == 0, 1, 0)
    near = 1 - far
    sent = (sent_rows(far), sent_rows(near))

    def swap_copies(kind):
        plan = [(field.at[kind], 4, (patch, other))]
        for way in (near, far):
            neighbour = jnp.where(way == 1, before, after)
            plan = [
                (picked.at[kind, way], 2 * way, (neighbour, core)),
                (picked.at[kind, way], 2 * way + 1, (neighbour, other)),
            ] + plan
        return [
            pltpu.make_async_remote_copy(
                src_ref=source,
                dst_ref=landed.at[kind, slot],
                send_sem=swap_send.at[kind, slot],
                recv_sem=swap_recv.at[kind, slot],
                device_id=target,
                device_id_type=MESH,
            )
            for source, slot, target in plan
        ]

    def start_swap(kind):
        copies = swap_copies(kind)
        for turn, way in enumerate((far, near)):
            for o in range(NB):
                row, mine = sent[turn][o]
                picked[kind, way, o] = field[kind, row] * mine
            for copy in copies[2 * turn : 2 * turn + 2]:
                copy.start()
        copies[4].start()

    def sum_copies(parity, phase):
        return [
            pltpu.make_async_remote_copy(
                src_ref=dots.at[parity, phase],
                dst_ref=landed_dots.at[parity, phase, offset],
                send_sem=sum_send.at[parity, phase],
                recv_sem=sum_recv.at[parity, phase],
                device_id=member(phase, offset),
                device_id_type=MESH,
            )
            for offset in offsets[phase]
        ]

    def all_sums(parity, phase):
        rows = landed_dots.at[parity, phase, pl.ds(1, counts[phase] - 1)]
        return pltpu.make_async_remote_copy(
            src_ref=rows,
            dst_ref=rows,
            send_sem=sum_send.at[parity, phase],
            recv_sem=sum_recv.at[parity, phase],
            device_id=(patch, other),
            device_id_type=MESH,
        )

    def finish_sum(parity, phase):
        all_sums(parity, phase).wait_recv()
        rows = [dots[parity, phase]]
        rows += [landed_dots[parity, phase, offset] for offset in range(1, counts[phase])]
        while len(rows) > 1:
            rows = [sum(rows[k : k + 2][1:], rows[k]) for k in range(0, len(rows), 2)]
        return rows[0]

    def end_sends(copies):
        for copy in copies:
            copy.wait_send()

    def landing(kind, slot):
        return pltpu.make_async_remote_copy(
            src_ref=landed.at[kind, slot],
            dst_ref=landed.at[kind, slot],
            send_sem=swap_send.at[kind, slot],
            recv_sem=swap_recv.at[kind, slot],
            device_id=(patch, other),
            device_id_type=MESH,
        )

    def own_blocks(kind):
        return [field[kind, s] for s in range(NB)]

    def core_blocks(kind):
        landing(kind, 4).wait_recv()
        return [landed[kind, 4, s] for s in range(NB)]

    def margin_blocks(kind, way):
        landing(kind, 2 * way).wait_recv()
        landing(kind, 2 * way + 1).wait_recv()
        return [landed[kind, 2 * way, o] + landed[kind, 2 * way + 1, o] for o in range(NB)]

    def apply_first():
        for base, values in (
            (first_slot, own_blocks(0)),
            (other * NB, core_blocks(0)),
            (PB + NB * far, margin_blocks(0, far)),
            (PB + NB * near, margin_blocks(0, near)),
        ):
            for o in range(NB):
                ext_parts[base + o] = vector_parts(values[o])
        for b in range(NB):
            gathered = jnp.concatenate([ext_parts[cols_ref[b, k]] for k in range(NEAR)], axis=1)
            full = jnp.dot(gathered, mixed_w[b], preferred_element_type=F32)
            field[1, b] = gather_parts(full) * live[b]

    def apply_group(weights, base, values):
        parts = jnp.concatenate([vector_parts(value) for value in values], axis=1)
        rows = pl.ds(pl.multiple_of(base * BS, NB * BS), NB * BS)
        full = jnp.dot(parts, weights[rows, :], preferred_element_type=F32)
        width = full.shape[1] // NB
        return [gather_parts(full[:, width * b : width * (b + 1)]) for b in range(NB)]

    def apply_dense(kind, weights, meanwhile):
        total = apply_group(weights, first_slot, own_blocks(kind))
        part = apply_group(weights, other * NB, core_blocks(kind))
        total = [total[b] + part[b] for b in range(NB)]
        part = apply_group(weights, PB + NB * far, margin_blocks(kind, far))
        total = [total[b] + part[b] for b in range(NB)]
        meanwhile()
        part = apply_group(weights, PB + NB * near, margin_blocks(kind, near))
        for b in range(NB):
            field[1 - kind, b] = total[b] + part[b]

    def make_dense(weights, blocks, turned):
        @pl.loop(0, NE)
        def _(e):
            rows = pl.ds(pl.multiple_of(e * BS, BS), BS)
            for b in range(NB):
                total = jnp.zeros((BS, BS), F32)
                for k in range(NEAR):
                    total = total + blocks[b, k] * jnp.where(cols_ref[b, k] == e, live[b], 0.0)
                if not turned:
                    total = total.T
                width = weights.shape[1] // NB
                columns = slice(width * b, width * (b + 1))
                weights[rows, columns] = matrix_parts(total, 1, width // BS)

    def dot_lanes(pairs, first=0):
        tile = jnp.zeros((ROWS, BS), F32)
        for q, (left, right) in enumerate(pairs, first):
            partial = left[0] * right[0]
            for s in range(1, NB):
                partial = partial + left[s] * right[s]
            total = jnp.sum(partial, axis=1, keepdims=True)
            tile = jnp.where(lane == q * ROWS + case, total, tile)
        return tile

    def in_row(tile):
        return jnp.sum(tile, axis=0, keepdims=True)

    def pick(tile, q):
        mine = jnp.where(lane == q * ROWS + case, jnp.broadcast_to(tile, (ROWS, BS)), 0.0)
        return jnp.broadcast_to(jnp.sum(mine, axis=1, keepdims=True), (ROWS, BS))

    loads[0].wait()
    empty = jnp.zeros((ROWS - NRHS, BS), F32)
    for s in range(NB):
        value = jnp.concatenate([right_in[:, s, :], empty], axis=0) * live[s]
        field[0, s] = value
        state[0, s] = value
    pl.semaphore_wait(barrier, greeted)
    start_swap(0)
    loads[1].wait()
    for e in range(NE):
        inverse_parts[e] = matrix_parts(inverse_in[e], 1)

    @pl.loop(0, NB)
    def _(b):
        pltpu.make_async_copy(near_ref.at[b], near_in.at[b], load_sem.at[2 + b]).wait()
        own = inverse_in[first_slot + b]
        own_parts = matrix_parts(own, 0)
        for k in range(NEAR):
            rows = slice(k * BS, (k + 1) * BS)
            block = near_in[b, k]
            left = matrix_product(own_parts, matrix_parts(block, 1))
            value = -matrix_product(matrix_parts(left, 0), inverse_parts[cols_ref[b, k]])
            if k == 0:
                value = 2.0 * own + value
            value = value.T
            mixed_in[b, k] = value
            mixed_w[b, rows, :] = matrix_parts(value, 1, 3)

    R, RAW1, Z1, FIRST, ZETA1, MAPPED1, SECOND, ZETA2, MAPPED2, RAWZ, RAWM, SOL, PART = range(13)
    NORM, INVERSE, SQUARE, COSINE, SINE, INVERSE_RADIUS, FACTOR = range(7)

    def get(index):
        return [state[index, s] for s in range(NB)]

    def put(index, values):
        for s in range(NB):
            state[index, s] = values[s]

    def of_field(kind):
        return [field[kind, s] for s in range(NB)]

    def combine(*terms):
        out = []
        for s in range(NB):
            value = None
            for coefficient, vector in terms:
                term = vector[s] if coefficient is None else coefficient * vector[s]
                value = term if value is None else value + term
            out.append(value)
        return out

    def lead(total):
        square, mixed, mapped_square = [pick(total, q) for q in range(3)]
        norm = jnp.sqrt(square + EPSILON)
        inverse = 1.0 / norm
        first_square = square * inverse * inverse
        lead_dot = mixed * inverse * inverse
        reduced = mapped_square * inverse * inverse - lead_dot * lead_dot * (2.0 - first_square)
        lead_norm = jnp.sqrt(jnp.maximum(reduced, 0.0) + EPSILON)
        scale = 1.0 / lead_norm
        inverse_radius = 1.0 / jnp.sqrt(lead_dot * lead_dot + lead_norm * lead_norm)
        for index, value in (
            (NORM, norm),
            (INVERSE, inverse),
            (SQUARE, first_square),
            (COSINE, lead_dot * inverse_radius),
            (SINE, lead_norm * inverse_radius),
            (INVERSE_RADIUS, inverse_radius),
        ):
            scalars[index] = value
        first = combine((inverse, get(R)))
        mapped_one = combine((inverse, get(RAW1)))
        zeta_one = combine((inverse, get(Z1)))
        raw_zeta = combine((inverse, of_field(1)))
        second = combine((scale, combine((None, mapped_one), (-lead_dot, first))))
        put(FIRST, first)
        put(MAPPED1, mapped_one)
        put(ZETA1, zeta_one)
        put(RAWZ, raw_zeta)
        put(SECOND, second)
        put(ZETA2, combine((scale, combine((None, raw_zeta), (-lead_dot, zeta_one)))))
        scalars[FACTOR] = -scale * inverse
        put(PART, combine((-scale * lead_dot, mapped_one)))
        early[...] = dot_lanes([(first, second), (second, second)], 3)

    def coefficients(total):
        upper, lower, square, cross, second_square = [pick(total, q) for q in range(5)]
        tail = (
            square
            - upper * upper * (2.0 - scalars[SQUARE])
            - lower * lower * (2.0 - second_square)
            + 2.0 * upper * lower * cross
        )
        norm, cosine, sine = scalars[NORM], scalars[COSINE], scalars[SINE]
        carried = cosine * upper + sine * lower
        rotated = cosine * lower - sine * upper
        square_two = rotated * rotated + (jnp.maximum(tail, 0.0) + EPSILON)
        coef_two = -norm * sine * rotated / square_two
        coef_one = (norm * cosine - carried * coef_two) * scalars[INVERSE_RADIUS]
        return coef_one, coef_two

    def restart(total):
        one, two = coefficients(total)
        norm = scalars[NORM]
        mapped_one, zeta_one = get(MAPPED1), get(ZETA1)
        put(SOL, combine((one, zeta_one), (two, get(ZETA2))))
        put(R, combine((None, get(R)), (-one, mapped_one), (-two, get(MAPPED2))))
        put(Z1, combine((norm, zeta_one), (-one, get(RAWZ)), (-two, of_field(1))))
        put(PART, combine((norm, mapped_one), (-one, get(RAWM))))
        scalars[FACTOR] = two

    @pl.loop(0, 2 * CYCLES)
    def _(i):
        parity = lax.rem(i, 2)

        def pass_sum():
            dots[parity, 1] = finish_sum(parity, 0)
            for copy in sum_copies(parity, 1):
                copy.start()
            all_sums(parity, 0).wait_send()

        def use_sum():
            @pl.when(parity == 1)
            def _():
                lead(finish_sum(1, 1))
                all_sums(1, 1).wait_send()

            @pl.when(i == 2)
            def _():
                restart(finish_sum(0, 1))
                all_sums(0, 1).wait_send()

        @pl.when(i == 0)
        def _():
            apply_first()

        @pl.when(i >= 1)
        def _():
            apply_dense(0, mixed_dense, pass_sum)

        start_swap(1)
        end_sends(swap_copies(0))

        @pl.when(i == 0)
        def _():
            make_dense(near_dense, near_in, False)
            put(Z1, of_field(1))

        apply_dense(1, near_dense, use_sum)

        @pl.when(i >= 1)
        def _():
            mapped = of_field(0)
            put(RAWM, combine((scalars[INVERSE], mapped)))
            mapped = combine((None, get(PART)), (-scalars[FACTOR], mapped))
            for s in range(NB):
                field[0, s] = mapped[s]

        @pl.when(i < 2 * CYCLES - 1)
        def _():
            start_swap(0)

        @pl.when(parity == 0)
        def _():
            mapped, current = of_field(0), get(R)
            dots[1, 0] = in_row(
                dot_lanes([(current, current), (current, mapped), (mapped, mapped)])
            )
            for copy in sum_copies(1, 0):
                copy.start()
            put(RAW1, mapped)

        @pl.when(parity == 1)
        def _():
            mapped = of_field(0)
            dots[0, 0] = in_row(
                dot_lanes([(mapped, get(FIRST)), (mapped, get(SECOND)), (mapped, mapped)])
                + early[...]
            )
            for copy in sum_copies(0, 0):
                copy.start()
            put(MAPPED2, mapped)

        end_sends(swap_copies(1))

        @pl.when(i == 0)
        def _():
            make_dense(mixed_dense, mixed_in, True)

    dots[0, 1] = finish_sum(0, 0)
    for copy in sum_copies(0, 1):
        copy.start()
    all_sums(0, 0).wait_send()
    one, two = coefficients(finish_sum(0, 1))
    answer = combine((None, get(SOL)), (one, get(ZETA1)), (two, get(ZETA2)))
    left = combine((None, get(R)), (-one, get(MAPPED1)), (-two, get(MAPPED2)))
    for s in range(NB):
        both_ref[0, :, s, :] = answer[s][0:NRHS]
        both_ref[1, :, s, :] = left[s][0:NRHS]
    all_sums(0, 1).wait_send()


def factors(patches):
    known = {128: (4, 8, 4), 8: (2, 2, 2), 4: (1, 2, 2)}
    return known.get(patches, (1, patches, 1))


def local(shape, right_side, patch_blocks, send_rows, near_cols, near_blocks, inverses):
    counts = (2 * shape[1], shape[0] * shape[2])
    most = max(counts)
    field = jax.ShapeDtypeStruct((2,) + right_side.shape, F32)
    vmem = pl.BlockSpec(memory_space=pltpu.VMEM)
    hbm = pl.BlockSpec(memory_space=pltpu.HBM)
    send_rows, near_cols, right_side, near_blocks, inverses = [
        pltpu.with_memory_space_constraint(value, pltpu.HBM)
        for value in (send_rows, near_cols, right_side, near_blocks, inverses)
    ]
    both = pl.pallas_call(
        functools.partial(kernel, shape),
        out_shape=field,
        in_specs=[pl.BlockSpec(memory_space=pltpu.SMEM)] + [hbm] * 5,
        out_specs=vmem,
        scratch_shapes=[
            pltpu.SMEM((1, 2, NB), jnp.int32),
            pltpu.SMEM((NB, NEAR), jnp.int32),
            pltpu.VMEM((NRHS, NB, BS), F32),
            pltpu.VMEM((NB, NEAR, BS, BS), F32),
            pltpu.VMEM((NE, BS, BS), F32),
            pltpu.VMEM((NB, NEAR, BS, BS), F32),
            pltpu.VMEM((NB, NEAR * BS, 3 * BS), BF16),
            pltpu.VMEM((NE * BS, NB * 2 * BS), BF16),
            pltpu.VMEM((NE * BS, NB * 3 * BS), BF16),
            pltpu.VMEM((NE, BS, 2 * BS), BF16),
            pltpu.VMEM((NE, 32, BS), BF16),
            pltpu.VMEM((2, NB, ROWS, BS), F32),
            pltpu.VMEM((2, 2, NB, ROWS, BS), F32),
            pltpu.VMEM((2, 5, NB, ROWS, BS), F32),
            pltpu.VMEM((2, 2, 1, BS), F32),
            pltpu.VMEM((2, 2, most, 1, BS), F32),
            pltpu.VMEM((13, NB, ROWS, BS), F32),
            pltpu.VMEM((7, ROWS, BS), F32),
            pltpu.VMEM((ROWS, BS), F32),
            pltpu.SemaphoreType.DMA((4 + NB,)),
            pltpu.SemaphoreType.DMA((2, 5)),
            pltpu.SemaphoreType.DMA((2, 5)),
            pltpu.SemaphoreType.DMA((2, 2)),
            pltpu.SemaphoreType.DMA((2, 2)),
        ],
        compiler_params=pltpu.CompilerParams(
            collective_id=0, has_side_effects=True, vmem_limit_bytes=32 * 1024 * 1024
        ),
        name="gmres",
    )(patch_blocks, send_rows, near_cols, right_side, near_blocks, inverses)
    return both[0], both[1]


def solution(mesh):
    in_specs = (
        P(None, ("patch", "grp"), None),
        P("patch"),
        P("patch", None, None),
        P(("patch", "grp"), None),
        P(("patch", "grp"), None, None, None),
        P("patch", None, None, None),
    )
    out_specs = (P(None, ("patch", "grp"), None), P(None, ("patch", "grp"), None))
    shape = factors(mesh.shape["patch"])
    return jax.shard_map(
        functools.partial(local, shape),
        mesh=mesh,
        in_specs=in_specs,
        out_specs=out_specs,
        check_vma=False,
    )
```

```python
import functools

import jax
import jax.numpy as jnp
from jax import lax
from jax.experimental import pallas as pl
from jax.experimental.pallas import tpu as pltpu
from jax.sharding import PartitionSpec as P

CYCLES = 2
EPSILON = 1e-06
NB = 4
PB = 8
NE = 16
NEAR = 10
BS = 128
NRHS = 6
ROWS = 8
MESH = pl.DeviceIdType.MESH
F32 = jnp.float32
BF16 = jnp.bfloat16


def split_three(value):
    high = value.astype(BF16).astype(F32)
    rest = value - high
    middle = rest.astype(BF16).astype(F32)
    return high, middle, rest - middle


def vector_parts(value):
    high, middle, low = split_three(value)
    first = jnp.concatenate([high, middle], axis=0).astype(BF16)
    second = jnp.concatenate([low, jnp.zeros_like(low)], axis=0).astype(BF16)
    return jnp.concatenate([first, second], axis=0)


def matrix_parts(value, axis, count=2):
    parts = []
    for _ in range(count):
        parts.append(value.astype(BF16))
        value = value - parts[-1].astype(F32)
    return jnp.concatenate(parts, axis=axis)


def matrix_product(left, right):
    full = jnp.dot(left, right, preferred_element_type=F32)
    cross = full[0:BS, BS : 2 * BS] + full[BS : 2 * BS, 0:BS] + full[BS : 2 * BS, BS : 2 * BS]
    return full[0:BS, 0:BS] + cross


def gather_parts(full):
    high, middle, low = full[0:8], full[8:16], full[16:24]
    smallest = low[:, 0:BS] + middle[:, BS : 2 * BS]
    if full.shape[1] == 3 * BS:
        smallest = smallest + high[:, 2 * BS : 3 * BS]
    return high[:, 0:BS] + (middle[:, 0:BS] + high[:, BS : 2 * BS] + smallest)


def kernel(
    shape,
    blocks_ref,
    rows_hbm,
    cols_hbm,
    right_ref,
    near_ref,
    inverse_ref,
    both_ref,
    rows_ref,
    cols_ref,
    right_in,
    near_in,
    inverse_in,
    mixed_in,
    mixed_w,
    near_dense,
    mixed_dense,
    inverse_parts,
    ext_parts,
    field,
    picked,
    landed,
    dots,
    landed_dots,
    state,
    scalars,
    early,
    load_sem,
    swap_send,
    swap_recv,
    sum_send,
    sum_recv,
):
    size_x, size_z, size_y = shape
    patches = size_x * size_z * size_y
    patch = lax.axis_index("patch")
    core = lax.axis_index("grp")
    place_y = lax.rem(patch, size_y)
    place_z = lax.rem(lax.div(patch, size_y), size_z)
    place_x = lax.div(patch, size_y * size_z)
    before = lax.rem(patch + (patches - 1), patches)
    after = lax.rem(patch + 1, patches)
    other = 1 - core

    counts = (2 * size_z, size_x * size_y)

    def hops(offset, size):
        return min(offset, size - offset)

    offsets = (
        sorted(range(1, counts[0]), key=lambda o: -hops(o, counts[0])),
        sorted(
            range(1, counts[1]),
            key=lambda o: -hops(o // size_y, size_x) - hops(o % size_y, size_y),
        ),
    )

    def member(phase, offset):
        if phase == 0:
            place = lax.rem(place_z * 2 + core + offset, counts[0])
            spot_z, spot_core = lax.div(place, 2), lax.rem(place, 2)
            return ((place_x * size_z + spot_z) * size_y + place_y, spot_core)
        place = lax.rem(place_x * size_y + place_y + offset, counts[1])
        spot_x, spot_y = lax.div(place, size_y), lax.rem(place, size_y)
        return ((spot_x * size_z + place_z) * size_y + spot_y, core)

    landed[...] = jnp.zeros_like(landed)
    barrier = pltpu.get_barrier_semaphore()
    greeted = 0
    for target in ((patch, other), (before, core), (before, other), (after, core), (after, other)):
        pl.semaphore_signal(barrier, inc=1, device_id=target, device_id_type=MESH)
        greeted += 1
    loads = [pltpu.make_async_copy(right_ref, right_in, load_sem.at[0])]
    loads += [pltpu.make_async_copy(inverse_ref.at[0], inverse_in, load_sem.at[1])]
    loads += [
        pltpu.make_async_copy(near_ref.at[b], near_in.at[b], load_sem.at[2 + b])
        for b in range(NB)
    ]
    loads += [
        pltpu.make_async_copy(source, target, load_sem.at[2 + NB + i])
        for i, (source, target) in enumerate(((rows_hbm, rows_ref), (cols_hbm, cols_ref)))
    ]
    for load in loads[2 + NB :] + loads[: 2 + NB]:
        load.start()

    for phase in range(2):
        for offset in offsets[phase]:
            pl.semaphore_signal(
                barrier, inc=1, device_id=member(phase, offset), device_id_type=MESH
            )
            greeted += 1

    for load in loads[2 + NB :]:
        load.wait()
    first_slot = core * NB
    live = [
        jnp.where(first_slot + s < blocks_ref[0], jnp.float32(1), jnp.float32(0))
        for s in range(NB)
    ]
    lane = lax.broadcasted_iota(jnp.int32, (ROWS, BS), 1)
    case = lax.broadcasted_iota(jnp.int32, (ROWS, BS), 0)

    def sent_rows(way):
        found = []
        for o in range(NB):
            row = rows_ref[0, way, o]
            inside = jnp.logical_and(row >= first_slot, row < first_slot + NB)
            found.append(
                (jnp.bitwise_and(row, NB - 1), jnp.where(inside, jnp.float32(1), jnp.float32(0)))
            )
        return found

    far = jnp.where(place_y == 0, 1, 0)
    near = 1 - far
    sent = (sent_rows(far), sent_rows(near))

    def swap_copies(kind):
        cases = pl.ds(0, NRHS)
        plan = [(field.at[kind, :, cases], 4, (patch, other))]
        for way in (near, far):
            neighbour = jnp.where(way == 1, before, after)
            plan = [
                (picked.at[kind, way, :, cases], 2 * way, (neighbour, core)),
                (picked.at[kind, way, :, cases], 2 * way + 1, (neighbour, other)),
            ] + plan
        return [
            pltpu.make_async_remote_copy(
                src_ref=source,
                dst_ref=landed.at[kind, slot, :, cases],
                send_sem=swap_send.at[kind, slot],
                recv_sem=swap_recv.at[kind, slot],
                device_id=target,
                device_id_type=MESH,
            )
            for source, slot, target in plan
        ]

    def start_swap(kind):
        copies = swap_copies(kind)
        for turn, way in enumerate((far, near)):
            for o in range(NB):
                row, mine = sent[turn][o]
                picked[kind, way, o] = field[kind, row] * mine
            for copy in copies[2 * turn : 2 * turn + 2]:
                copy.start()
        copies[4].start()

    def sum_copies(parity, phase):
        return [
            pltpu.make_async_remote_copy(
                src_ref=dots.at[parity, phase],
                dst_ref=landed_dots.at[parity, phase, offset],
                send_sem=sum_send.at[parity, phase],
                recv_sem=sum_recv.at[parity, phase],
                device_id=member(phase, offset),
                device_id_type=MESH,
            )
            for offset in offsets[phase]
        ]

    def all_sums(parity, phase):
        rows = landed_dots.at[parity, phase, pl.ds(1, counts[phase] - 1)]
        return pltpu.make_async_remote_copy(
            src_ref=rows,
            dst_ref=rows,
            send_sem=sum_send.at[parity, phase],
            recv_sem=sum_recv.at[parity, phase],
            device_id=(patch, other),
            device_id_type=MESH,
        )

    def finish_sum(parity, phase):
        all_sums(parity, phase).wait_recv()
        rows = [dots[parity, phase]]
        rows += [landed_dots[parity, phase, offset] for offset in range(1, counts[phase])]
        while len(rows) > 1:
            rows = [sum(rows[k : k + 2][1:], rows[k]) for k in range(0, len(rows), 2)]
        return rows[0]

    def end_sends(copies):
        for copy in copies:
            copy.wait_send()

    def landing(kind, slot):
        blocks = landed.at[kind, slot, :, pl.ds(0, NRHS)]
        return pltpu.make_async_remote_copy(
            src_ref=blocks,
            dst_ref=blocks,
            send_sem=swap_send.at[kind, slot],
            recv_sem=swap_recv.at[kind, slot],
            device_id=(patch, other),
            device_id_type=MESH,
        )

    def own_blocks(kind):
        return [field[kind, s] for s in range(NB)]

    def core_blocks(kind):
        landing(kind, 4).wait_recv()
        return [landed[kind, 4, s] for s in range(NB)]

    def margin_blocks(kind, way):
        landing(kind, 2 * way).wait_recv()
        landing(kind, 2 * way + 1).wait_recv()
        return [landed[kind, 2 * way, o] + landed[kind, 2 * way + 1, o] for o in range(NB)]

    def apply_first():
        for base, values in (
            (first_slot, own_blocks(0)),
            (other * NB, core_blocks(0)),
            (PB + NB * far, margin_blocks(0, far)),
            (PB + NB * near, margin_blocks(0, near)),
        ):
            for o in range(NB):
                ext_parts[base + o] = vector_parts(values[o])
        for b in range(NB):
            gathered = jnp.concatenate([ext_parts[cols_ref[b, k]] for k in range(NEAR)], axis=1)
            full = jnp.dot(gathered, mixed_w[b], preferred_element_type=F32)
            field[1, b] = gather_parts(full) * live[b]

    def apply_group(weights, base, values):
        parts = jnp.concatenate([vector_parts(value) for value in values], axis=1)
        rows = pl.ds(pl.multiple_of(base * BS, NB * BS), NB * BS)
        full = jnp.dot(parts, weights[rows, :], preferred_element_type=F32)
        width = full.shape[1] // NB
        return [gather_parts(full[:, width * b : width * (b + 1)]) for b in range(NB)]

    def apply_dense(kind, weights, meanwhile):
        total = apply_group(weights, first_slot, own_blocks(kind))
        part = apply_group(weights, other * NB, core_blocks(kind))
        total = [total[b] + part[b] for b in range(NB)]
        part = apply_group(weights, PB + NB * far, margin_blocks(kind, far))
        total = [total[b] + part[b] for b in range(NB)]
        meanwhile()
        part = apply_group(weights, PB + NB * near, margin_blocks(kind, near))
        for b in range(NB):
            field[1 - kind, b] = total[b] + part[b]

    def make_dense(weights, blocks, turned):
        @pl.loop(0, NE)
        def _(e):
            rows = pl.ds(pl.multiple_of(e * BS, BS), BS)
            for b in range(NB):
                total = jnp.zeros((BS, BS), F32)
                for k in range(NEAR):
                    total = total + blocks[b, k] * jnp.where(cols_ref[b, k] == e, live[b], 0.0)
                if not turned:
                    total = total.T
                width = weights.shape[1] // NB
                columns = slice(width * b, width * (b + 1))
                weights[rows, columns] = matrix_parts(total, 1, width // BS)

    def dot_lanes(pairs, first=0):
        tile = jnp.zeros((ROWS, BS), F32)
        for q, (left, right) in enumerate(pairs, first):
            partial = left[0] * right[0]
            for s in range(1, NB):
                partial = partial + left[s] * right[s]
            total = jnp.sum(partial, axis=1, keepdims=True)
            tile = jnp.where(lane == q * ROWS + case, total, tile)
        return tile

    def in_row(tile):
        return jnp.sum(tile, axis=0, keepdims=True)

    def pick(tile, q):
        mine = jnp.where(lane == q * ROWS + case, jnp.broadcast_to(tile, (ROWS, BS)), 0.0)
        return jnp.broadcast_to(jnp.sum(mine, axis=1, keepdims=True), (ROWS, BS))

    loads[0].wait()
    empty = jnp.zeros((ROWS - NRHS, BS), F32)
    for s in range(NB):
        value = jnp.concatenate([right_in[:, s, :], empty], axis=0) * live[s]
        field[0, s] = value
        state[0, s] = value
    pl.semaphore_wait(barrier, greeted)
    start_swap(0)
    loads[1].wait()
    for e in range(NE):
        inverse_parts[e] = matrix_parts(inverse_in[e], 1)

    @pl.loop(0, NB)
    def _(b):
        pltpu.make_async_copy(near_ref.at[b], near_in.at[b], load_sem.at[2 + b]).wait()
        own = inverse_in[first_slot + b]
        own_parts = matrix_parts(own, 0)
        for k in range(NEAR):
            rows = slice(k * BS, (k + 1) * BS)
            block = near_in[b, k]
            left = matrix_product(own_parts, matrix_parts(block, 1))
            value = -matrix_product(matrix_parts(left, 0), inverse_parts[cols_ref[b, k]])
            if k == 0:
                value = 2.0 * own + value
            value = value.T
            mixed_in[b, k] = value
            mixed_w[b, rows, :] = matrix_parts(value, 1, 3)

    R, RAW1, Z1, FIRST, ZETA1, MAPPED1, SECOND, ZETA2, MAPPED2, RAWZ, RAWM, SOL, PART = range(13)
    NORM, INVERSE, SQUARE, COSINE, SINE, INVERSE_RADIUS, FACTOR = range(7)

    def get(index):
        return [state[index, s] for s in range(NB)]

    def put(index, values):
        for s in range(NB):
            state[index, s] = values[s]

    def of_field(kind):
        return [field[kind, s] for s in range(NB)]

    def combine(*terms):
        out = []
        for s in range(NB):
            value = None
            for coefficient, vector in terms:
                term = vector[s] if coefficient is None else coefficient * vector[s]
                value = term if value is None else value + term
            out.append(value)
        return out

    def lead(total):
        square, mixed, mapped_square = [pick(total, q) for q in range(3)]
        norm = jnp.sqrt(square + EPSILON)
        inverse = 1.0 / norm
        first_square = square * inverse * inverse
        lead_dot = mixed * inverse * inverse
        reduced = mapped_square * inverse * inverse - lead_dot * lead_dot * (2.0 - first_square)
        lead_norm = jnp.sqrt(jnp.maximum(reduced, 0.0) + EPSILON)
        scale = 1.0 / lead_norm
        inverse_radius = 1.0 / jnp.sqrt(lead_dot * lead_dot + lead_norm * lead_norm)
        for index, value in (
            (NORM, norm),
            (INVERSE, inverse),
            (SQUARE, first_square),
            (COSINE, lead_dot * inverse_radius),
            (SINE, lead_norm * inverse_radius),
            (INVERSE_RADIUS, inverse_radius),
        ):
            scalars[index] = value
        first = combine((inverse, get(R)))
        mapped_one = combine((inverse, get(RAW1)))
        zeta_one = combine((inverse, get(Z1)))
        raw_zeta = combine((inverse, of_field(1)))
        second = combine((scale, combine((None, mapped_one), (-lead_dot, first))))
        put(FIRST, first)
        put(MAPPED1, mapped_one)
        put(ZETA1, zeta_one)
        put(RAWZ, raw_zeta)
        put(SECOND, second)
        put(ZETA2, combine((scale, combine((None, raw_zeta), (-lead_dot, zeta_one)))))
        scalars[FACTOR] = -scale * inverse
        put(PART, combine((-scale * lead_dot, mapped_one)))
        early[...] = dot_lanes([(first, second), (second, second)], 3)

    def coefficients(total):
        upper, lower, square, cross, second_square = [pick(total, q) for q in range(5)]
        tail = (
            square
            - upper * upper * (2.0 - scalars[SQUARE])
            - lower * lower * (2.0 - second_square)
            + 2.0 * upper * lower * cross
        )
        norm, cosine, sine = scalars[NORM], scalars[COSINE], scalars[SINE]
        carried = cosine * upper + sine * lower
        rotated = cosine * lower - sine * upper
        square_two = rotated * rotated + (jnp.maximum(tail, 0.0) + EPSILON)
        coef_two = -norm * sine * rotated / square_two
        coef_one = (norm * cosine - carried * coef_two) * scalars[INVERSE_RADIUS]
        return coef_one, coef_two

    def restart(total):
        one, two = coefficients(total)
        norm = scalars[NORM]
        mapped_one, zeta_one = get(MAPPED1), get(ZETA1)
        put(SOL, combine((one, zeta_one), (two, get(ZETA2))))
        put(R, combine((None, get(R)), (-one, mapped_one), (-two, get(MAPPED2))))
        put(Z1, combine((norm, zeta_one), (-one, get(RAWZ)), (-two, of_field(1))))
        put(PART, combine((norm, mapped_one), (-one, get(RAWM))))
        scalars[FACTOR] = two

    @pl.loop(0, 2 * CYCLES)
    def _(i):
        parity = lax.rem(i, 2)

        def pass_sum():
            dots[parity, 1] = finish_sum(parity, 0)
            for copy in sum_copies(parity, 1):
                copy.start()
            all_sums(parity, 0).wait_send()

        def use_sum():
            @pl.when(parity == 1)
            def _():
                lead(finish_sum(1, 1))
                all_sums(1, 1).wait_send()

            @pl.when(i == 2)
            def _():
                restart(finish_sum(0, 1))
                all_sums(0, 1).wait_send()

        @pl.when(i == 0)
        def _():
            apply_first()

        @pl.when(i >= 1)
        def _():
            apply_dense(0, mixed_dense, pass_sum)

        start_swap(1)
        end_sends(swap_copies(0))

        @pl.when(i == 0)
        def _():
            make_dense(near_dense, near_in, False)
            put(Z1, of_field(1))

        apply_dense(1, near_dense, use_sum)

        @pl.when(i >= 1)
        def _():
            mapped = of_field(0)
            put(RAWM, combine((scalars[INVERSE], mapped)))
            mapped = combine((None, get(PART)), (-scalars[FACTOR], mapped))
            for s in range(NB):
                field[0, s] = mapped[s]

        @pl.when(i < 2 * CYCLES - 1)
        def _():
            start_swap(0)

        @pl.when(parity == 0)
        def _():
            mapped, current = of_field(0), get(R)
            dots[1, 0] = in_row(
                dot_lanes([(current, current), (current, mapped), (mapped, mapped)])
            )
            for copy in sum_copies(1, 0):
                copy.start()
            put(RAW1, mapped)

        @pl.when(parity == 1)
        def _():
            mapped = of_field(0)
            dots[0, 0] = in_row(
                dot_lanes([(mapped, get(FIRST)), (mapped, get(SECOND)), (mapped, mapped)])
                + early[...]
            )
            for copy in sum_copies(0, 0):
                copy.start()
            put(MAPPED2, mapped)

        end_sends(swap_copies(1))

        @pl.when(i == 0)
        def _():
            make_dense(mixed_dense, mixed_in, True)

    dots[0, 1] = finish_sum(0, 0)
    for copy in sum_copies(0, 1):
        copy.start()
    all_sums(0, 0).wait_send()
    one, two = coefficients(finish_sum(0, 1))
    answer = combine((None, get(SOL)), (one, get(ZETA1)), (two, get(ZETA2)))
    left = combine((None, get(R)), (-one, get(MAPPED1)), (-two, get(MAPPED2)))
    for s in range(NB):
        both_ref[0, :, s, :] = answer[s][0:NRHS]
        both_ref[1, :, s, :] = left[s][0:NRHS]
    all_sums(0, 1).wait_send()


def factors(patches):
    known = {128: (4, 8, 4), 8: (2, 2, 2), 4: (1, 2, 2)}
    return known.get(patches, (1, patches, 1))


def local(shape, right_side, patch_blocks, send_rows, near_cols, near_blocks, inverses):
    counts = (2 * shape[1], shape[0] * shape[2])
    most = max(counts)
    field = jax.ShapeDtypeStruct((2,) + right_side.shape, F32)
    vmem = pl.BlockSpec(memory_space=pltpu.VMEM)
    hbm = pl.BlockSpec(memory_space=pltpu.HBM)
    send_rows, near_cols, right_side, near_blocks, inverses = [
        pltpu.with_memory_space_constraint(value, pltpu.HBM)
        for value in (send_rows, near_cols, right_side, near_blocks, inverses)
    ]
    both = pl.pallas_call(
        functools.partial(kernel, shape),
        out_shape=field,
        in_specs=[pl.BlockSpec(memory_space=pltpu.SMEM)] + [hbm] * 5,
        out_specs=vmem,
        scratch_shapes=[
            pltpu.SMEM((1, 2, NB), jnp.int32),
            pltpu.SMEM((NB, NEAR), jnp.int32),
            pltpu.VMEM((NRHS, NB, BS), F32),
            pltpu.VMEM((NB, NEAR, BS, BS), F32),
            pltpu.VMEM((NE, BS, BS), F32),
            pltpu.VMEM((NB, NEAR, BS, BS), F32),
            pltpu.VMEM((NB, NEAR * BS, 3 * BS), BF16),
            pltpu.VMEM((NE * BS, NB * 2 * BS), BF16),
            pltpu.VMEM((NE * BS, NB * 3 * BS), BF16),
            pltpu.VMEM((NE, BS, 2 * BS), BF16),
            pltpu.VMEM((NE, 32, BS), BF16),
            pltpu.VMEM((2, NB, ROWS, BS), F32),
            pltpu.VMEM((2, 2, NB, ROWS, BS), F32),
            pltpu.VMEM((2, 5, NB, ROWS, BS), F32),
            pltpu.VMEM((2, 2, 1, BS), F32),
            pltpu.VMEM((2, 2, most, 1, BS), F32),
            pltpu.VMEM((13, NB, ROWS, BS), F32),
            pltpu.VMEM((7, ROWS, BS), F32),
            pltpu.VMEM((ROWS, BS), F32),
            pltpu.SemaphoreType.DMA((4 + NB,)),
            pltpu.SemaphoreType.DMA((2, 5)),
            pltpu.SemaphoreType.DMA((2, 5)),
            pltpu.SemaphoreType.DMA((2, 2)),
            pltpu.SemaphoreType.DMA((2, 2)),
        ],
        compiler_params=pltpu.CompilerParams(
            collective_id=0, has_side_effects=True, vmem_limit_bytes=32 * 1024 * 1024
        ),
        name="gmres",
    )(patch_blocks, send_rows, near_cols, right_side, near_blocks, inverses)
    return both[0], both[1]


def solution(mesh):
    in_specs = (
        P(None, ("patch", "grp"), None),
        P("patch"),
        P("patch", None, None),
        P(("patch", "grp"), None),
        P(("patch", "grp"), None, None, None),
        P("patch", None, None, None),
    )
    out_specs = (P(None, ("patch", "grp"), None), P(None, ("patch", "grp"), None))
    shape = factors(mesh.shape["patch"])
    return jax.shard_map(
        functools.partial(local, shape),
        mesh=mesh,
        in_specs=in_specs,
        out_specs=out_specs,
        check_vma=False,
    )
```

```python
import functools

import jax
import jax.numpy as jnp
from jax import lax
from jax.experimental import pallas as pl
from jax.experimental.pallas import tpu as pltpu
from jax.sharding import PartitionSpec as P

CYCLES = 2
EPSILON = 1e-06
NB = 4
PB = 8
NE = 16
NEAR = 10
BS = 128
NRHS = 6
ROWS = 8
MESH = pl.DeviceIdType.MESH
F32 = jnp.float32
BF16 = jnp.bfloat16


def split_three(value):
    high = value.astype(BF16).astype(F32)
    rest = value - high
    middle = rest.astype(BF16).astype(F32)
    return high, middle, rest - middle


def vector_parts(value):
    high, middle, low = split_three(value)
    first = jnp.concatenate([high, middle], axis=0).astype(BF16)
    second = jnp.concatenate([low, jnp.zeros_like(low)], axis=0).astype(BF16)
    return jnp.concatenate([first, second], axis=0)


def matrix_parts(value, axis, count=2):
    parts = []
    for _ in range(count):
        parts.append(value.astype(BF16))
        value = value - parts[-1].astype(F32)
    return jnp.concatenate(parts, axis=axis)


def matrix_product(left, right):
    full = jnp.dot(left, right, preferred_element_type=F32)
    cross = full[0:BS, BS : 2 * BS] + full[BS : 2 * BS, 0:BS] + full[BS : 2 * BS, BS : 2 * BS]
    return full[0:BS, 0:BS] + cross


def gather_parts(full):
    high, middle, low = full[0:8], full[8:16], full[16:24]
    smallest = low[:, 0:BS] + middle[:, BS : 2 * BS]
    if full.shape[1] == 3 * BS:
        smallest = smallest + high[:, 2 * BS : 3 * BS]
    return high[:, 0:BS] + (middle[:, 0:BS] + high[:, BS : 2 * BS] + smallest)


def kernel(
    shape,
    blocks_ref,
    rows_hbm,
    cols_hbm,
    right_ref,
    near_ref,
    inverse_ref,
    both_ref,
    rows_ref,
    cols_ref,
    right_in,
    near_in,
    inverse_in,
    mixed_in,
    mixed_w,
    near_dense,
    mixed_dense,
    inverse_parts,
    ext_parts,
    field,
    picked,
    landed,
    dots,
    landed_dots,
    state,
    scalars,
    early,
    load_sem,
    swap_send,
    swap_recv,
    sum_send,
    sum_recv,
):
    size_x, size_z, size_y = shape
    patches = size_x * size_z * size_y
    patch = lax.axis_index("patch")
    core = lax.axis_index("grp")
    place_y = lax.rem(patch, size_y)
    place_z = lax.rem(lax.div(patch, size_y), size_z)
    place_x = lax.div(patch, size_y * size_z)
    before = lax.rem(patch + (patches - 1), patches)
    after = lax.rem(patch + 1, patches)
    other = 1 - core

    counts = (2 * size_z, size_x * size_y)

    def hops(offset, size):
        return min(offset, size - offset)

    offsets = (
        sorted(range(1, counts[0]), key=lambda o: -hops(o, counts[0])),
        sorted(
            range(1, counts[1]),
            key=lambda o: -hops(o // size_y, size_x) - hops(o % size_y, size_y),
        ),
    )

    def member(phase, offset):
        if phase == 0:
            place = lax.rem(place_z * 2 + core + offset, counts[0])
            spot_z, spot_core = lax.div(place, 2), lax.rem(place, 2)
            return ((place_x * size_z + spot_z) * size_y + place_y, spot_core)
        place = lax.rem(place_x * size_y + place_y + offset, counts[1])
        spot_x, spot_y = lax.div(place, size_y), lax.rem(place, size_y)
        return ((spot_x * size_z + place_z) * size_y + spot_y, core)

    barrier = pltpu.get_barrier_semaphore()
    loads = [pltpu.make_async_copy(right_ref, right_in, load_sem.at[0])]
    loads += [pltpu.make_async_copy(inverse_ref.at[0], inverse_in, load_sem.at[1])]
    loads += [
        pltpu.make_async_copy(near_ref.at[b], near_in.at[b], load_sem.at[2 + b])
        for b in range(NB)
    ]
    loads += [
        pltpu.make_async_copy(source, target, load_sem.at[2 + NB + i])
        for i, (source, target) in enumerate(((rows_hbm, rows_ref), (cols_hbm, cols_ref)))
    ]
    for load in loads[2 + NB :] + loads[:1]:
        load.start()
    greeted = 0
    for target in ((patch, other), (before, core), (before, other), (after, core), (after, other)):
        pl.semaphore_signal(barrier, inc=1, device_id=target, device_id_type=MESH)
        greeted += 1
    for load in loads[1 : 2 + NB]:
        load.start()

    for phase in range(2):
        for offset in offsets[phase]:
            pl.semaphore_signal(
                barrier, inc=1, device_id=member(phase, offset), device_id_type=MESH
            )
            greeted += 1

    for load in loads[2 + NB :]:
        load.wait()
    first_slot = core * NB
    live = [
        jnp.where(first_slot + s < blocks_ref[0], jnp.float32(1), jnp.float32(0))
        for s in range(NB)
    ]
    lane = lax.broadcasted_iota(jnp.int32, (ROWS, BS), 1)
    case = lax.broadcasted_iota(jnp.int32, (ROWS, BS), 0)

    def sent_rows(way):
        found = []
        for o in range(NB):
            row = rows_ref[0, way, o]
            inside = jnp.logical_and(row >= first_slot, row < first_slot + NB)
            found.append(
                (jnp.bitwise_and(row, NB - 1), jnp.where(inside, jnp.float32(1), jnp.float32(0)))
            )
        return found

    far = jnp.where(place_y == 0, 1, 0)
    near = 1 - far
    sent = (sent_rows(far), sent_rows(near))

    def swap_copies(kind):
        plan = [(field.at[kind], 4, (patch, other))]
        for way in (near, far):
            neighbour = jnp.where(way == 1, before, after)
            plan = [
                (picked.at[kind, way], 2 * way, (neighbour, core)),
                (picked.at[kind, way], 2 * way + 1, (neighbour, other)),
            ] + plan
        return [
            pltpu.make_async_remote_copy(
                src_ref=source,
                dst_ref=landed.at[kind, slot],
                send_sem=swap_send.at[kind, slot],
                recv_sem=swap_recv.at[kind, slot],
                device_id=target,
                device_id_type=MESH,
            )
            for source, slot, target in plan
        ]

    def start_swap(kind):
        copies = swap_copies(kind)
        for turn, way in enumerate((far, near)):
            for o in range(NB):
                row, mine = sent[turn][o]
                picked[kind, way, o] = field[kind, row] * mine
            for copy in copies[2 * turn : 2 * turn + 2]:
                copy.start()
        copies[4].start()

    def sum_copies(parity, phase):
        return [
            pltpu.make_async_remote_copy(
                src_ref=dots.at[parity, phase],
                dst_ref=landed_dots.at[parity, phase, offset],
                send_sem=sum_send.at[parity, phase],
                recv_sem=sum_recv.at[parity, phase],
                device_id=member(phase, offset),
                device_id_type=MESH,
            )
            for offset in offsets[phase]
        ]

    def all_sums(parity, phase):
        rows = landed_dots.at[parity, phase, pl.ds(1, counts[phase] - 1)]
        return pltpu.make_async_remote_copy(
            src_ref=rows,
            dst_ref=rows,
            send_sem=sum_send.at[parity, phase],
            recv_sem=sum_recv.at[parity, phase],
            device_id=(patch, other),
            device_id_type=MESH,
        )

    def finish_sum(parity, phase):
        all_sums(parity, phase).wait_recv()
        rows = [dots[parity, phase]]
        rows += [landed_dots[parity, phase, offset] for offset in range(1, counts[phase])]
        while len(rows) > 1:
            rows = [sum(rows[k : k + 2][1:], rows[k]) for k in range(0, len(rows), 2)]
        return rows[0]

    def end_sends(copies):
        for copy in copies:
            copy.wait_send()

    def landing(kind, slot):
        return pltpu.make_async_remote_copy(
            src_ref=landed.at[kind, slot],
            dst_ref=landed.at[kind, slot],
            send_sem=swap_send.at[kind, slot],
            recv_sem=swap_recv.at[kind, slot],
            device_id=(patch, other),
            device_id_type=MESH,
        )

    def own_blocks(kind):
        return [field[kind, s] for s in range(NB)]

    def core_blocks(kind):
        landing(kind, 4).wait_recv()
        return [landed[kind, 4, s] for s in range(NB)]

    def margin_blocks(kind, way):
        landing(kind, 2 * way).wait_recv()
        landing(kind, 2 * way + 1).wait_recv()
        return [landed[kind, 2 * way, o] + landed[kind, 2 * way + 1, o] for o in range(NB)]

    def apply_first():
        for base, values in (
            (first_slot, own_blocks(0)),
            (other * NB, core_blocks(0)),
            (PB + NB * far, margin_blocks(0, far)),
            (PB + NB * near, margin_blocks(0, near)),
        ):
            for o in range(NB):
                ext_parts[base + o] = vector_parts(values[o])
        for b in range(NB):
            gathered = jnp.concatenate([ext_parts[cols_ref[b, k]] for k in range(NEAR)], axis=1)
            full = jnp.dot(gathered, mixed_w[b], preferred_element_type=F32)
            field[1, b] = gather_parts(full) * live[b]

    def apply_group(weights, base, values):
        parts = jnp.concatenate([vector_parts(value) for value in values], axis=1)
        rows = pl.ds(pl.multiple_of(base * BS, NB * BS), NB * BS)
        full = jnp.dot(parts, weights[rows, :], preferred_element_type=F32)
        width = full.shape[1] // NB
        return [gather_parts(full[:, width * b : width * (b + 1)]) for b in range(NB)]

    def apply_dense(kind, weights, meanwhile, finish):
        total = apply_group(weights, first_slot, own_blocks(kind))
        part = apply_group(weights, other * NB, core_blocks(kind))
        total = [total[b] + part[b] for b in range(NB)]
        part = apply_group(weights, PB + NB * far, margin_blocks(kind, far))
        total = [total[b] + part[b] for b in range(NB)]
        meanwhile()
        part = apply_group(weights, PB + NB * near, margin_blocks(kind, near))
        for b in range(NB):
            field[1 - kind, b] = finish(b, total[b] + part[b])

    def make_dense(weights, blocks, turned):
        @pl.loop(0, NE)
        def _(e):
            rows = pl.ds(pl.multiple_of(e * BS, BS), BS)
            for b in range(NB):
                total = jnp.zeros((BS, BS), F32)
                for k in range(NEAR):
                    total = total + blocks[b, k] * jnp.where(cols_ref[b, k] == e, live[b], 0.0)
                if not turned:
                    total = total.T
                width = weights.shape[1] // NB
                columns = slice(width * b, width * (b + 1))
                weights[rows, columns] = matrix_parts(total, 1, width // BS)

    def dot_lanes(pairs, first=0):
        tile = jnp.zeros((ROWS, BS), F32)
        for q, (left, right) in enumerate(pairs, first):
            partial = left[0] * right[0]
            for s in range(1, NB):
                partial = partial + left[s] * right[s]
            total = jnp.sum(partial, axis=1, keepdims=True)
            tile = jnp.where(lane == q * ROWS + case, total, tile)
        return tile

    def in_row(tile):
        return jnp.sum(tile, axis=0, keepdims=True)

    def pick(tile, q):
        mine = jnp.where(lane == q * ROWS + case, jnp.broadcast_to(tile, (ROWS, BS)), 0.0)
        return jnp.broadcast_to(jnp.sum(mine, axis=1, keepdims=True), (ROWS, BS))

    loads[0].wait()
    empty = jnp.zeros((ROWS - NRHS, BS), F32)
    for s in range(NB):
        value = jnp.concatenate([right_in[:, s, :], empty], axis=0) * live[s]
        field[0, s] = value
        state[0, s] = value
    pl.semaphore_wait(barrier, greeted)
    start_swap(0)
    loads[1].wait()
    for e in range(NE):
        inverse_parts[e] = matrix_parts(inverse_in[e], 1)

    @pl.loop(0, NB)
    def _(b):
        pltpu.make_async_copy(near_ref.at[b], near_in.at[b], load_sem.at[2 + b]).wait()
        own = inverse_in[first_slot + b]
        own_parts = matrix_parts(own, 0)
        for k in range(NEAR):
            rows = slice(k * BS, (k + 1) * BS)
            block = near_in[b, k]
            left = matrix_product(own_parts, matrix_parts(block, 1))
            value = -matrix_product(matrix_parts(left, 0), inverse_parts[cols_ref[b, k]])
            if k == 0:
                value = 2.0 * own + value
            value = value.T
            mixed_in[b, k] = value
            mixed_w[b, rows, :] = matrix_parts(value, 1, 3)

    R, RAW1, Z1, FIRST, ZETA1, MAPPED1, SECOND, ZETA2, MAPPED2, RAWZ, RAWM, SOL, PART = range(13)
    NORM, INVERSE, SQUARE, COSINE, SINE, INVERSE_RADIUS, FACTOR = range(7)

    def get(index):
        return [state[index, s] for s in range(NB)]

    def put(index, values):
        for s in range(NB):
            state[index, s] = values[s]

    def of_field(kind):
        return [field[kind, s] for s in range(NB)]

    def combine(*terms):
        out = []
        for s in range(NB):
            value = None
            for coefficient, vector in terms:
                term = vector[s] if coefficient is None else coefficient * vector[s]
                value = term if value is None else value + term
            out.append(value)
        return out

    def lead(total):
        square, mixed, mapped_square = [pick(total, q) for q in range(3)]
        norm = jnp.sqrt(square + EPSILON)
        inverse = 1.0 / norm
        first_square = square * inverse * inverse
        lead_dot = mixed * inverse * inverse
        reduced = mapped_square * inverse * inverse - lead_dot * lead_dot * (2.0 - first_square)
        lead_norm = jnp.sqrt(jnp.maximum(reduced, 0.0) + EPSILON)
        scale = 1.0 / lead_norm
        inverse_radius = 1.0 / jnp.sqrt(lead_dot * lead_dot + lead_norm * lead_norm)
        for index, value in (
            (NORM, norm),
            (INVERSE, inverse),
            (SQUARE, first_square),
            (COSINE, lead_dot * inverse_radius),
            (SINE, lead_norm * inverse_radius),
            (INVERSE_RADIUS, inverse_radius),
        ):
            scalars[index] = value
        first = combine((inverse, get(R)))
        mapped_one = combine((inverse, get(RAW1)))
        zeta_one = combine((inverse, get(Z1)))
        raw_zeta = combine((inverse, of_field(1)))
        second = combine((scale, combine((None, mapped_one), (-lead_dot, first))))
        put(FIRST, first)
        put(MAPPED1, mapped_one)
        put(ZETA1, zeta_one)
        put(RAWZ, raw_zeta)
        put(SECOND, second)
        put(ZETA2, combine((scale, combine((None, raw_zeta), (-lead_dot, zeta_one)))))
        scalars[FACTOR] = -scale * inverse
        put(PART, combine((-scale * lead_dot, mapped_one)))
        early[...] = dot_lanes([(first, second), (second, second)], 3)

    def coefficients(total):
        upper, lower, square, cross, second_square = [pick(total, q) for q in range(5)]
        tail = (
            square
            - upper * upper * (2.0 - scalars[SQUARE])
            - lower * lower * (2.0 - second_square)
            + 2.0 * upper * lower * cross
        )
        norm, cosine, sine = scalars[NORM], scalars[COSINE], scalars[SINE]
        carried = cosine * upper + sine * lower
        rotated = cosine * lower - sine * upper
        square_two = rotated * rotated + (jnp.maximum(tail, 0.0) + EPSILON)
        coef_two = -norm * sine * rotated / square_two
        coef_one = (norm * cosine - carried * coef_two) * scalars[INVERSE_RADIUS]
        return coef_one, coef_two

    def restart(total):
        one, two = coefficients(total)
        norm = scalars[NORM]
        mapped_one, zeta_one = get(MAPPED1), get(ZETA1)
        put(SOL, combine((one, zeta_one), (two, get(ZETA2))))
        put(R, combine((None, get(R)), (-one, mapped_one), (-two, get(MAPPED2))))
        put(Z1, combine((norm, zeta_one), (-one, get(RAWZ)), (-two, of_field(1))))
        put(PART, combine((norm, mapped_one), (-one, get(RAWM))))
        scalars[FACTOR] = two

    state[PART] = jnp.zeros((NB, ROWS, BS), F32)
    scalars[INVERSE] = jnp.zeros((ROWS, BS), F32)
    scalars[FACTOR] = jnp.full((ROWS, BS), -1.0, F32)

    @pl.loop(0, 2 * CYCLES)
    def _(i):
        parity = lax.rem(i, 2)

        def pass_sum():
            dots[parity, 1] = finish_sum(parity, 0)
            for copy in sum_copies(parity, 1):
                copy.start()
            all_sums(parity, 0).wait_send()

        def use_sum():
            @pl.when(parity == 1)
            def _():
                lead(finish_sum(1, 1))
                all_sums(1, 1).wait_send()

            @pl.when(i == 2)
            def _():
                restart(finish_sum(0, 1))
                all_sums(0, 1).wait_send()

        @pl.when(i == 0)
        def _():
            apply_first()

        @pl.when(i >= 1)
        def _():
            apply_dense(0, mixed_dense, pass_sum, lambda b, value: value)

        start_swap(1)
        end_sends(swap_copies(0))

        @pl.when(i == 0)
        def _():
            make_dense(near_dense, near_in, False)
            put(Z1, of_field(1))

        def to_next(b, value):
            state[RAWM, b] = scalars[INVERSE] * value
            return state[PART, b] - scalars[FACTOR] * value

        apply_dense(1, near_dense, use_sum, to_next)

        @pl.when(i < 2 * CYCLES - 1)
        def _():
            start_swap(0)

        @pl.when(parity == 0)
        def _():
            mapped, current = of_field(0), get(R)
            dots[1, 0] = in_row(
                dot_lanes([(current, current), (current, mapped), (mapped, mapped)])
            )
            for copy in sum_copies(1, 0):
                copy.start()
            put(RAW1, mapped)

        @pl.when(parity == 1)
        def _():
            mapped = of_field(0)
            dots[0, 0] = in_row(
                dot_lanes([(mapped, get(FIRST)), (mapped, get(SECOND)), (mapped, mapped)])
                + early[...]
            )
            for copy in sum_copies(0, 0):
                copy.start()
            put(MAPPED2, mapped)

        end_sends(swap_copies(1))

        @pl.when(i == 0)
        def _():
            make_dense(mixed_dense, mixed_in, True)

    dots[0, 1] = finish_sum(0, 0)
    for copy in sum_copies(0, 1):
        copy.start()
    all_sums(0, 0).wait_send()
    one, two = coefficients(finish_sum(0, 1))
    answer = combine((None, get(SOL)), (one, get(ZETA1)), (two, get(ZETA2)))
    left = combine((None, get(R)), (-one, get(MAPPED1)), (-two, get(MAPPED2)))
    for s in range(NB):
        both_ref[0, :, s, :] = answer[s][0:NRHS]
        both_ref[1, :, s, :] = left[s][0:NRHS]
    all_sums(0, 1).wait_send()


def factors(patches):
    known = {128: (4, 8, 4), 8: (2, 2, 2), 4: (1, 2, 2)}
    return known.get(patches, (1, patches, 1))


def local(shape, right_side, patch_blocks, send_rows, near_cols, near_blocks, inverses):
    counts = (2 * shape[1], shape[0] * shape[2])
    most = max(counts)
    field = jax.ShapeDtypeStruct((2,) + right_side.shape, F32)
    vmem = pl.BlockSpec(memory_space=pltpu.VMEM)
    hbm = pl.BlockSpec(memory_space=pltpu.HBM)
    send_rows, near_cols, right_side, near_blocks, inverses = [
        pltpu.with_memory_space_constraint(value, pltpu.HBM)
        for value in (send_rows, near_cols, right_side, near_blocks, inverses)
    ]
    both = pl.pallas_call(
        functools.partial(kernel, shape),
        out_shape=field,
        in_specs=[pl.BlockSpec(memory_space=pltpu.SMEM)] + [hbm] * 5,
        out_specs=vmem,
        scratch_shapes=[
            pltpu.SMEM((1, 2, NB), jnp.int32),
            pltpu.SMEM((NB, NEAR), jnp.int32),
            pltpu.VMEM((NRHS, NB, BS), F32),
            pltpu.VMEM((NB, NEAR, BS, BS), F32),
            pltpu.VMEM((NE, BS, BS), F32),
            pltpu.VMEM((NB, NEAR, BS, BS), F32),
            pltpu.VMEM((NB, NEAR * BS, 3 * BS), BF16),
            pltpu.VMEM((NE * BS, NB * 2 * BS), BF16),
            pltpu.VMEM((NE * BS, NB * 3 * BS), BF16),
            pltpu.VMEM((NE, BS, 2 * BS), BF16),
            pltpu.VMEM((NE, 32, BS), BF16),
            pltpu.VMEM((2, NB, ROWS, BS), F32),
            pltpu.VMEM((2, 2, NB, ROWS, BS), F32),
            pltpu.VMEM((2, 5, NB, ROWS, BS), F32),
            pltpu.VMEM((2, 2, 1, BS), F32),
            pltpu.VMEM((2, 2, most, 1, BS), F32),
            pltpu.VMEM((13, NB, ROWS, BS), F32),
            pltpu.VMEM((7, ROWS, BS), F32),
            pltpu.VMEM((ROWS, BS), F32),
            pltpu.SemaphoreType.DMA((4 + NB,)),
            pltpu.SemaphoreType.DMA((2, 5)),
            pltpu.SemaphoreType.DMA((2, 5)),
            pltpu.SemaphoreType.DMA((2, 2)),
            pltpu.SemaphoreType.DMA((2, 2)),
        ],
        compiler_params=pltpu.CompilerParams(
            collective_id=0, has_side_effects=True, vmem_limit_bytes=32 * 1024 * 1024
        ),
        name="gmres",
    )(patch_blocks, send_rows, near_cols, right_side, near_blocks, inverses)
    return both[0], both[1]


def solution(mesh):
    in_specs = (
        P(None, ("patch", "grp"), None),
        P("patch"),
        P("patch", None, None),
        P(("patch", "grp"), None),
        P(("patch", "grp"), None, None, None),
        P("patch", None, None, None),
    )
    out_specs = (P(None, ("patch", "grp"), None), P(None, ("patch", "grp"), None))
    shape = factors(mesh.shape["patch"])
    return jax.shard_map(
        functools.partial(local, shape),
        mesh=mesh,
        in_specs=in_specs,
        out_specs=out_specs,
        check_vma=False,
    )
```

```python
import functools

import jax
import jax.numpy as jnp
from jax import lax
from jax.experimental import pallas as pl
from jax.experimental.pallas import tpu as pltpu
from jax.sharding import PartitionSpec as P

CYCLES = 2
EPSILON = 1e-06
NB = 4
PB = 8
NE = 16
NEAR = 10
BS = 128
NRHS = 6
ROWS = 8
MESH = pl.DeviceIdType.MESH
F32 = jnp.float32
BF16 = jnp.bfloat16


def split_three(value):
    high = value.astype(BF16).astype(F32)
    rest = value - high
    middle = rest.astype(BF16).astype(F32)
    return high, middle, rest - middle


def vector_parts(value):
    high, middle, low = split_three(value)
    first = jnp.concatenate([high, middle], axis=0).astype(BF16)
    second = jnp.concatenate([low, jnp.zeros_like(low)], axis=0).astype(BF16)
    return jnp.concatenate([first, second], axis=0)


def matrix_parts(value, axis, count=2):
    parts = []
    for _ in range(count):
        parts.append(value.astype(BF16))
        value = value - parts[-1].astype(F32)
    return jnp.concatenate(parts, axis=axis)


def matrix_product(left, right):
    full = jnp.dot(left, right, preferred_element_type=F32)
    cross = full[0:BS, BS : 2 * BS] + full[BS : 2 * BS, 0:BS] + full[BS : 2 * BS, BS : 2 * BS]
    return full[0:BS, 0:BS] + cross


def gather_parts(full):
    high, middle, low = full[0:8], full[8:16], full[16:24]
    smallest = low[:, 0:BS] + middle[:, BS : 2 * BS]
    if full.shape[1] == 3 * BS:
        smallest = smallest + high[:, 2 * BS : 3 * BS]
    return high[:, 0:BS] + (middle[:, 0:BS] + high[:, BS : 2 * BS] + smallest)


def kernel(
    shape,
    blocks_ref,
    rows_hbm,
    cols_hbm,
    right_ref,
    near_ref,
    inverse_ref,
    both_ref,
    rows_ref,
    cols_ref,
    right_in,
    near_in,
    inverse_in,
    mixed_in,
    mixed_w,
    near_dense,
    mixed_dense,
    inverse_parts,
    ext_parts,
    field,
    picked,
    landed,
    dots,
    landed_dots,
    state,
    scalars,
    early,
    load_sem,
    swap_send,
    swap_recv,
    sum_send,
    sum_recv,
):
    size_x, size_z, size_y = shape
    patches = size_x * size_z * size_y
    patch = lax.axis_index("patch")
    core = lax.axis_index("grp")
    place_y = lax.rem(patch, size_y)
    place_z = lax.rem(lax.div(patch, size_y), size_z)
    place_x = lax.div(patch, size_y * size_z)
    before = lax.rem(patch + (patches - 1), patches)
    after = lax.rem(patch + 1, patches)
    other = 1 - core

    counts = (2 * size_z, size_x * size_y)

    def hops(offset, size):
        return min(offset, size - offset)

    offsets = (
        sorted(range(1, counts[0]), key=lambda o: -hops(o, counts[0])),
        sorted(
            range(1, counts[1]),
            key=lambda o: -hops(o // size_y, size_x) - hops(o % size_y, size_y),
        ),
    )

    def member(phase, offset):
        if phase == 0:
            place = lax.rem(place_z * 2 + core + offset, counts[0])
            spot_z, spot_core = lax.div(place, 2), lax.rem(place, 2)
            return ((place_x * size_z + spot_z) * size_y + place_y, spot_core)
        place = lax.rem(place_x * size_y + place_y + offset, counts[1])
        spot_x, spot_y = lax.div(place, size_y), lax.rem(place, size_y)
        return ((spot_x * size_z + place_z) * size_y + spot_y, core)

    landed[...] = jnp.zeros_like(landed)
    barrier = pltpu.get_barrier_semaphore()
    greeted = 0
    for target in ((patch, other), (before, core), (before, other), (after, core), (after, other)):
        pl.semaphore_signal(barrier, inc=1, device_id=target, device_id_type=MESH)
        greeted += 1
    loads = [pltpu.make_async_copy(right_ref, right_in, load_sem.at[0])]
    loads += [pltpu.make_async_copy(inverse_ref.at[0], inverse_in, load_sem.at[1])]
    loads += [
        pltpu.make_async_copy(near_ref.at[b], near_in.at[b], load_sem.at[2 + b])
        for b in range(NB)
    ]
    loads += [
        pltpu.make_async_copy(source, target, load_sem.at[2 + NB + i])
        for i, (source, target) in enumerate(((rows_hbm, rows_ref), (cols_hbm, cols_ref)))
    ]
    for load in loads[2 + NB :] + loads[: 2 + NB]:
        load.start()

    for phase in range(2):
        for offset in offsets[phase]:
            pl.semaphore_signal(
                barrier, inc=1, device_id=member(phase, offset), device_id_type=MESH
            )
            greeted += 1

    for load in loads[2 + NB :]:
        load.wait()
    first_slot = core * NB
    live = [
        jnp.where(first_slot + s < blocks_ref[0], jnp.float32(1), jnp.float32(0))
        for s in range(NB)
    ]
    lane = lax.broadcasted_iota(jnp.int32, (ROWS, BS), 1)
    case = lax.broadcasted_iota(jnp.int32, (ROWS, BS), 0)

    def sent_rows(way):
        found = []
        for o in range(NB):
            row = rows_ref[0, way, o]
            inside = jnp.logical_and(row >= first_slot, row < first_slot + NB)
            found.append(
                (jnp.bitwise_and(row, NB - 1), jnp.where(inside, jnp.float32(1), jnp.float32(0)))
            )
        return found

    far = jnp.where(place_y == 0, 1, 0)
    near = 1 - far
    sent = (sent_rows(far), sent_rows(near))

    def swap_copies(kind):
        cases = pl.ds(0, NRHS)
        plan = [(field.at[kind, :, cases], 4, (patch, other))]
        for way in (near, far):
            neighbour = jnp.where(way == 1, before, after)
            plan = [
                (picked.at[kind, way, :, cases], 2 * way, (neighbour, core)),
                (picked.at[kind, way, :, cases], 2 * way + 1, (neighbour, other)),
            ] + plan
        return [
            pltpu.make_async_remote_copy(
                src_ref=source,
                dst_ref=landed.at[kind, slot, :, cases],
                send_sem=swap_send.at[kind, slot],
                recv_sem=swap_recv.at[kind, slot],
                device_id=target,
                device_id_type=MESH,
            )
            for source, slot, target in plan
        ]

    def start_swap(kind):
        copies = swap_copies(kind)
        for turn, way in enumerate((far, near)):
            for o in range(NB):
                row, mine = sent[turn][o]
                picked[kind, way, o] = field[kind, row] * mine
            for copy in copies[2 * turn : 2 * turn + 2]:
                copy.start()
        copies[4].start()

    def sum_copies(parity, phase):
        return [
            pltpu.make_async_remote_copy(
                src_ref=dots.at[parity, phase],
                dst_ref=landed_dots.at[parity, phase, offset],
                send_sem=sum_send.at[parity, phase],
                recv_sem=sum_recv.at[parity, phase],
                device_id=member(phase, offset),
                device_id_type=MESH,
            )
            for offset in offsets[phase]
        ]

    def all_sums(parity, phase):
        rows = landed_dots.at[parity, phase, pl.ds(1, counts[phase] - 1)]
        return pltpu.make_async_remote_copy(
            src_ref=rows,
            dst_ref=rows,
            send_sem=sum_send.at[parity, phase],
            recv_sem=sum_recv.at[parity, phase],
            device_id=(patch, other),
            device_id_type=MESH,
        )

    def finish_sum(parity, phase):
        all_sums(parity, phase).wait_recv()
        rows = [dots[parity, phase]]
        rows += [landed_dots[parity, phase, offset] for offset in range(1, counts[phase])]
        while len(rows) > 1:
            rows = [sum(rows[k : k + 2][1:], rows[k]) for k in range(0, len(rows), 2)]
        return rows[0]

    def end_sends(copies):
        for copy in copies:
            copy.wait_send()

    def landing(kind, slot):
        blocks = landed.at[kind, slot, :, pl.ds(0, NRHS)]
        return pltpu.make_async_remote_copy(
            src_ref=blocks,
            dst_ref=blocks,
            send_sem=swap_send.at[kind, slot],
            recv_sem=swap_recv.at[kind, slot],
            device_id=(patch, other),
            device_id_type=MESH,
        )

    def own_blocks(kind):
        return [field[kind, s] for s in range(NB)]

    def core_blocks(kind):
        landing(kind, 4).wait_recv()
        return [landed[kind, 4, s] for s in range(NB)]

    def margin_blocks(kind, way):
        landing(kind, 2 * way).wait_recv()
        landing(kind, 2 * way + 1).wait_recv()
        return [landed[kind, 2 * way, o] + landed[kind, 2 * way + 1, o] for o in range(NB)]

    def apply_first():
        for base, values in (
            (first_slot, own_blocks(0)),
            (other * NB, core_blocks(0)),
            (PB + NB * far, margin_blocks(0, far)),
            (PB + NB * near, margin_blocks(0, near)),
        ):
            for o in range(NB):
                ext_parts[base + o] = vector_parts(values[o])
        for b in range(NB):
            gathered = jnp.concatenate([ext_parts[cols_ref[b, k]] for k in range(NEAR)], axis=1)
            full = jnp.dot(gathered, mixed_w[b], preferred_element_type=F32)
            field[1, b] = gather_parts(full) * live[b]

    def apply_group(weights, base, values):
        parts = jnp.concatenate([vector_parts(value) for value in values], axis=1)
        rows = pl.ds(pl.multiple_of(base * BS, NB * BS), NB * BS)
        full = jnp.dot(parts, weights[rows, :], preferred_element_type=F32)
        width = full.shape[1] // NB
        return [gather_parts(full[:, width * b : width * (b + 1)]) for b in range(NB)]

    def apply_dense(kind, weights, meanwhile):
        total = apply_group(weights, first_slot, own_blocks(kind))
        part = apply_group(weights, other * NB, core_blocks(kind))
        total = [total[b] + part[b] for b in range(NB)]
        part = apply_group(weights, PB + NB * far, margin_blocks(kind, far))
        total = [total[b] + part[b] for b in range(NB)]
        meanwhile()
        part = apply_group(weights, PB + NB * near, margin_blocks(kind, near))
        for b in range(NB):
            field[1 - kind, b] = total[b] + part[b]

    def make_dense(weights, blocks, turned):
        @pl.loop(0, NE)
        def _(e):
            rows = pl.ds(pl.multiple_of(e * BS, BS), BS)
            for b in range(NB):
                total = jnp.zeros((BS, BS), F32)
                for k in range(NEAR):
                    total = total + blocks[b, k] * jnp.where(cols_ref[b, k] == e, live[b], 0.0)
                if not turned:
                    total = total.T
                width = weights.shape[1] // NB
                columns = slice(width * b, width * (b + 1))
                weights[rows, columns] = matrix_parts(total, 1, width // BS)

    def dot_lanes(pairs, first=0):
        tile = jnp.zeros((ROWS, BS), F32)
        for q, (left, right) in enumerate(pairs, first):
            partial = left[0] * right[0]
            for s in range(1, NB):
                partial = partial + left[s] * right[s]
            total = jnp.sum(partial, axis=1, keepdims=True)
            tile = jnp.where(lane == q * ROWS + case, total, tile)
        return tile

    def in_row(tile):
        return jnp.sum(tile, axis=0, keepdims=True)

    def pick(tile, q):
        mine = jnp.where(lane == q * ROWS + case, jnp.broadcast_to(tile, (ROWS, BS)), 0.0)
        return jnp.broadcast_to(jnp.sum(mine, axis=1, keepdims=True), (ROWS, BS))

    loads[0].wait()
    empty = jnp.zeros((ROWS - NRHS, BS), F32)
    for s in range(NB):
        value = jnp.concatenate([right_in[:, s, :], empty], axis=0) * live[s]
        field[0, s] = value
        state[0, s] = value
    pl.semaphore_wait(barrier, greeted)
    start_swap(0)
    loads[1].wait()
    for e in range(NE):
        inverse_parts[e] = matrix_parts(inverse_in[e], 1)

    @pl.loop(0, NB)
    def _(b):
        pltpu.make_async_copy(near_ref.at[b], near_in.at[b], load_sem.at[2 + b]).wait()
        own = inverse_in[first_slot + b]
        own_parts = matrix_parts(own, 0)
        for k in range(NEAR):
            rows = slice(k * BS, (k + 1) * BS)
            block = near_in[b, k]
            left = matrix_product(own_parts, matrix_parts(block, 1))
            value = -matrix_product(matrix_parts(left, 0), inverse_parts[cols_ref[b, k]])
            if k == 0:
                value = 2.0 * own + value
            value = value.T
            mixed_in[b, k] = value
            mixed_w[b, rows, :] = matrix_parts(value, 1, 3)

    R, RAW1, Z1, FIRST, ZETA1, MAPPED1, SECOND, ZETA2, MAPPED2, RAWZ, RAWM, SOL, PART = range(13)
    NORM, INVERSE, SQUARE, COSINE, SINE, INVERSE_RADIUS, FACTOR = range(7)

    def get(index):
        return [state[index, s] for s in range(NB)]

    def put(index, values):
        for s in range(NB):
            state[index, s] = values[s]

    def of_field(kind):
        return [field[kind, s] for s in range(NB)]

    def combine(*terms):
        out = []
        for s in range(NB):
            value = None
            for coefficient, vector in terms:
                term = vector[s] if coefficient is None else coefficient * vector[s]
                value = term if value is None else value + term
            out.append(value)
        return out

    def lead(total):
        square, mixed, mapped_square = [pick(total, q) for q in range(3)]
        norm = jnp.sqrt(square + EPSILON)
        inverse = 1.0 / norm
        first_square = square * inverse * inverse
        lead_dot = mixed * inverse * inverse
        reduced = mapped_square * inverse * inverse - lead_dot * lead_dot * (2.0 - first_square)
        lead_norm = jnp.sqrt(jnp.maximum(reduced, 0.0) + EPSILON)
        scale = 1.0 / lead_norm
        inverse_radius = 1.0 / jnp.sqrt(lead_dot * lead_dot + lead_norm * lead_norm)
        for index, value in (
            (NORM, norm),
            (INVERSE, inverse),
            (SQUARE, first_square),
            (COSINE, lead_dot * inverse_radius),
            (SINE, lead_norm * inverse_radius),
            (INVERSE_RADIUS, inverse_radius),
        ):
            scalars[index] = value
        first = combine((inverse, get(R)))
        mapped_one = combine((inverse, get(RAW1)))
        zeta_one = combine((inverse, get(Z1)))
        raw_zeta = combine((inverse, of_field(1)))
        second = combine((scale, combine((None, mapped_one), (-lead_dot, first))))
        put(FIRST, first)
        put(MAPPED1, mapped_one)
        put(ZETA1, zeta_one)
        put(RAWZ, raw_zeta)
        put(SECOND, second)
        put(ZETA2, combine((scale, combine((None, raw_zeta), (-lead_dot, zeta_one)))))
        scalars[FACTOR] = -scale * inverse
        put(PART, combine((-scale * lead_dot, mapped_one)))
        early[...] = dot_lanes([(first, second), (second, second)], 3)

    def coefficients(total):
        upper, lower, square, cross, second_square = [pick(total, q) for q in range(5)]
        tail = (
            square
            - upper * upper * (2.0 - scalars[SQUARE])
            - lower * lower * (2.0 - second_square)
            + 2.0 * upper * lower * cross
        )
        norm, cosine, sine = scalars[NORM], scalars[COSINE], scalars[SINE]
        carried = cosine * upper + sine * lower
        rotated = cosine * lower - sine * upper
        square_two = rotated * rotated + (jnp.maximum(tail, 0.0) + EPSILON)
        coef_two = -norm * sine * rotated / square_two
        coef_one = (norm * cosine - carried * coef_two) * scalars[INVERSE_RADIUS]
        return coef_one, coef_two

    def restart(total):
        one, two = coefficients(total)
        norm = scalars[NORM]
        mapped_one, zeta_one = get(MAPPED1), get(ZETA1)
        put(SOL, combine((one, zeta_one), (two, get(ZETA2))))
        put(R, combine((None, get(R)), (-one, mapped_one), (-two, get(MAPPED2))))
        put(Z1, combine((norm, zeta_one), (-one, get(RAWZ)), (-two, of_field(1))))
        put(PART, combine((norm, mapped_one), (-one, get(RAWM))))
        scalars[FACTOR] = two

    @pl.loop(0, 2 * CYCLES)
    def _(i):
        parity = lax.rem(i, 2)

        def pass_sum():
            dots[parity, 1] = finish_sum(parity, 0)
            for copy in sum_copies(parity, 1):
                copy.start()
            all_sums(parity, 0).wait_send()

        def use_sum():
            @pl.when(parity == 1)
            def _():
                lead(finish_sum(1, 1))
                all_sums(1, 1).wait_send()

            @pl.when(i == 2)
            def _():
                restart(finish_sum(0, 1))
                all_sums(0, 1).wait_send()

        @pl.when(i == 0)
        def _():
            apply_first()

        @pl.when(i >= 1)
        def _():
            apply_dense(0, mixed_dense, lambda: None)

        start_swap(1)

        @pl.when(i >= 1)
        def _():
            pass_sum()

        end_sends(swap_copies(0))

        @pl.when(i == 0)
        def _():
            make_dense(near_dense, near_in, False)
            put(Z1, of_field(1))

        apply_dense(1, near_dense, use_sum)

        @pl.when(i >= 1)
        def _():
            mapped = of_field(0)
            put(RAWM, combine((scalars[INVERSE], mapped)))
            mapped = combine((None, get(PART)), (-scalars[FACTOR], mapped))
            for s in range(NB):
                field[0, s] = mapped[s]

        @pl.when(i < 2 * CYCLES - 1)
        def _():
            start_swap(0)

        @pl.when(parity == 0)
        def _():
            mapped, current = of_field(0), get(R)
            dots[1, 0] = in_row(
                dot_lanes([(current, current), (current, mapped), (mapped, mapped)])
            )
            for copy in sum_copies(1, 0):
                copy.start()
            put(RAW1, mapped)

        @pl.when(parity == 1)
        def _():
            mapped = of_field(0)
            dots[0, 0] = in_row(
                dot_lanes([(mapped, get(FIRST)), (mapped, get(SECOND)), (mapped, mapped)])
                + early[...]
            )
            for copy in sum_copies(0, 0):
                copy.start()
            put(MAPPED2, mapped)

        end_sends(swap_copies(1))

        @pl.when(i == 0)
        def _():
            make_dense(mixed_dense, mixed_in, True)

    dots[0, 1] = finish_sum(0, 0)
    for copy in sum_copies(0, 1):
        copy.start()
    all_sums(0, 0).wait_send()
    one, two = coefficients(finish_sum(0, 1))
    answer = combine((None, get(SOL)), (one, get(ZETA1)), (two, get(ZETA2)))
    left = combine((None, get(R)), (-one, get(MAPPED1)), (-two, get(MAPPED2)))
    for s in range(NB):
        both_ref[0, :, s, :] = answer[s][0:NRHS]
        both_ref[1, :, s, :] = left[s][0:NRHS]
    all_sums(0, 1).wait_send()


def factors(patches):
    known = {128: (4, 8, 4), 8: (2, 2, 2), 4: (1, 2, 2)}
    return known.get(patches, (1, patches, 1))


def local(shape, right_side, patch_blocks, send_rows, near_cols, near_blocks, inverses):
    counts = (2 * shape[1], shape[0] * shape[2])
    most = max(counts)
    field = jax.ShapeDtypeStruct((2,) + right_side.shape, F32)
    vmem = pl.BlockSpec(memory_space=pltpu.VMEM)
    hbm = pl.BlockSpec(memory_space=pltpu.HBM)
    send_rows, near_cols, right_side, near_blocks, inverses = [
        pltpu.with_memory_space_constraint(value, pltpu.HBM)
        for value in (send_rows, near_cols, right_side, near_blocks, inverses)
    ]
    both = pl.pallas_call(
        functools.partial(kernel, shape),
        out_shape=field,
        in_specs=[pl.BlockSpec(memory_space=pltpu.SMEM)] + [hbm] * 5,
        out_specs=vmem,
        scratch_shapes=[
            pltpu.SMEM((1, 2, NB), jnp.int32),
            pltpu.SMEM((NB, NEAR), jnp.int32),
            pltpu.VMEM((NRHS, NB, BS), F32),
            pltpu.VMEM((NB, NEAR, BS, BS), F32),
            pltpu.VMEM((NE, BS, BS), F32),
            pltpu.VMEM((NB, NEAR, BS, BS), F32),
            pltpu.VMEM((NB, NEAR * BS, 3 * BS), BF16),
            pltpu.VMEM((NE * BS, NB * 2 * BS), BF16),
            pltpu.VMEM((NE * BS, NB * 3 * BS), BF16),
            pltpu.VMEM((NE, BS, 2 * BS), BF16),
            pltpu.VMEM((NE, 32, BS), BF16),
            pltpu.VMEM((2, NB, ROWS, BS), F32),
            pltpu.VMEM((2, 2, NB, ROWS, BS), F32),
            pltpu.VMEM((2, 5, NB, ROWS, BS), F32),
            pltpu.VMEM((2, 2, 1, BS), F32),
            pltpu.VMEM((2, 2, most, 1, BS), F32),
            pltpu.VMEM((13, NB, ROWS, BS), F32),
            pltpu.VMEM((7, ROWS, BS), F32),
            pltpu.VMEM((ROWS, BS), F32),
            pltpu.SemaphoreType.DMA((4 + NB,)),
            pltpu.SemaphoreType.DMA((2, 5)),
            pltpu.SemaphoreType.DMA((2, 5)),
            pltpu.SemaphoreType.DMA((2, 2)),
            pltpu.SemaphoreType.DMA((2, 2)),
        ],
        compiler_params=pltpu.CompilerParams(
            collective_id=0, has_side_effects=True, vmem_limit_bytes=32 * 1024 * 1024
        ),
        name="gmres",
    )(patch_blocks, send_rows, near_cols, right_side, near_blocks, inverses)
    return both[0], both[1]


def solution(mesh):
    in_specs = (
        P(None, ("patch", "grp"), None),
        P("patch"),
        P("patch", None, None),
        P(("patch", "grp"), None),
        P(("patch", "grp"), None, None, None),
        P("patch", None, None, None),
    )
    out_specs = (P(None, ("patch", "grp"), None), P(None, ("patch", "grp"), None))
    shape = factors(mesh.shape["patch"])
    return jax.shard_map(
        functools.partial(local, shape),
        mesh=mesh,
        in_specs=in_specs,
        out_specs=out_specs,
        check_vma=False,
    )
```
